32 devices in a mesh: blk: 8 (over z, x), frq: 4 (over y, core).
Axes of the slice: x: 2, y: 2, z: 4, core: 2. Of those that a mesh axis runs over, the one named last changes fastest.
Arguments:
- spectra: bfloat16 [2, 3, 128, 512], P(None, None, 'blk', 'frq'), may hold values from -6 to 6
- observed: bfloat16 [128, 3, 3, 1024], P(('blk', 'frq')), may hold values from -6 to 6
- own_station: int32 [8, 8, 2], P('blk'), may hold values from 0 to 15
- partner_station: int32 [8, 8, 2], P('blk'), may hold values from 0 to 15, as said below
- pair_count: int32 [8, 8], P('blk'), may hold values from 1 to 2, as said below
Outputs:
- adjoint: float32 [1024, 3, 128], P('frq', None, 'blk')
The draws below stay inside these ranges and needn't reach their ends.
Inputs may be any that keep to these rules, and one draw needn't show every extreme that they name: `partner_station`: within the reading block's own block pair, a slot's two stations differ. `pair_count`: the live slots of a block pair are its first ones; every reading block has a block pair with all 2 slots live.
All inputs are finite; a program needn't handle non-finite values.
Results may differ from the reference program's by a relative error of at most 0.003.
Values may be sent and summed in bfloat16 or wider, within the bound.
A program may use at most 64 MiB of HBM per device.

```python
import math
import jax
import jax.numpy as jnp
from jax import lax

STA_DEV = 16
CAP = 2
NF = 512
BLOCKS = 8
STATIONS = 128
PAIRS = 128
NT = 1024


def station_pairs(key):
    shape = (BLOCKS, BLOCKS, CAP)
    own_draw = jax.random.randint(jax.random.fold_in(key, 11), shape, 0, STA_DEV)
    other_draw = jax.random.randint(jax.random.fold_in(key, 12), shape, 0, STA_DEV)
    offset = jax.random.randint(jax.random.fold_in(key, 13), shape, 1, STA_DEV)
    diagonal = (jnp.arange(BLOCKS)[:, None] == jnp.arange(BLOCKS)[None, :])[:, :, None]
    partner = jnp.where(diagonal, (own_draw + offset) % STA_DEV, other_draw)
    return (own_draw.astype(jnp.int32), partner.astype(jnp.int32))


def draw_own_station(key, part):
    return station_pairs(key)[0]


def draw_partner_station(key, part):
    return station_pairs(key)[1]


def draw_pair_count(key, part):
    counts = jax.random.randint(jax.random.fold_in(key, 21), (BLOCKS, BLOCKS), 1, CAP + 1)
    full_pick = jax.random.randint(jax.random.fold_in(key, 22), (BLOCKS,), 0, BLOCKS)
    chosen = jnp.arange(BLOCKS)[None, :] == full_pick[:, None]
    return jnp.where(chosen, CAP, counts).astype(jnp.int32)


def block_levels(own_key, shape, cuts, smallest, high):
    loudness = 1.0
    for axis_at, blocks in cuts:
        draws = jax.random.uniform(jax.random.fold_in(jax.random.fold_in(own_key, 6), axis_at), (blocks,), jnp.float32, smallest / len(cuts), high / len(cuts))
        loudness = loudness * jnp.repeat(jnp.exp(draws), shape[axis_at] // blocks).reshape((-1,) + (1,) * (len(shape) - 1 - axis_at))
    return loudness


def gaussian(stream_key, shape, spread, limit, pieces=(), held_as=jnp.bfloat16):
    gain = block_levels(stream_key, shape, pieces, -0.22, 0.18) if pieces else 1.0
    drawn = jax.random.normal(stream_key, shape, jnp.float32) * spread * gain
    return jnp.minimum(jnp.maximum(drawn, -limit), limit).astype(held_as)


def setup_inputs(seed: int = 0) -> dict:
    seeds = jax.random.split(jax.random.key(seed), 6)
    return {
        "spectra": gaussian(seeds[0], (2, 3, STATIONS, NF), 1.0, 6.0, ((2, 8), (3, 4))),
        "observed": gaussian(seeds[1], (PAIRS, 3, 3, NT), 1.0, 6.0, ((0, 32),)),
        "own_station": draw_own_station(jax.random.fold_in(seeds[5], 71), 0),
        "partner_station": draw_partner_station(jax.random.fold_in(seeds[5], 71), 0),
        "pair_count": draw_pair_count(jax.random.fold_in(seeds[5], 71), 0),
    }


def phase_table(freq_start, freq_count, time_start, time_count):
    freq_index = lax.iota(jnp.int32, freq_count) + freq_start
    time_index = lax.iota(jnp.int32, time_count) + time_start
    phase_num = (2 * freq_index + 1)[:, None] * time_index[None, :] % (2 * NT)
    return phase_num.astype(jnp.float32) * (math.pi / NT)

def lag_window():
    time_index = lax.iota(jnp.int32, NT)
    lag_size = jnp.minimum(time_index, NT - time_index)
    return ((lag_size >= NT // 32) & (lag_size < NT // 4)).astype(jnp.float32)

def cross_spectra(first_rows, second_rows):
    real_part = first_rows[:, 0, :, None] * second_rows[:, 0, None, :] + first_rows[:, 1, :, None] * second_rows[:, 1, None, :]
    imag_part = first_rows[:, 1, :, None] * second_rows[:, 0, None, :] - first_rows[:, 0, :, None] * second_rows[:, 1, None, :]
    return jnp.stack([real_part, imag_part], axis=3)

def pair_gradients(adjoint_rows, first_rows, second_rows):
    adj_real = adjoint_rows[:, :, :, 0]
    adj_imag = adjoint_rows[:, :, :, 1]
    own_real = lax.optimization_barrier(jnp.sum(adj_real * second_rows[:, 0, None] - adj_imag * second_rows[:, 1, None], axis=2))
    own_imag = lax.optimization_barrier(jnp.sum(adj_real * second_rows[:, 1, None] + adj_imag * second_rows[:, 0, None], axis=2))
    far_real = lax.optimization_barrier(jnp.sum(adj_real * first_rows[:, 0, :, None] + adj_imag * first_rows[:, 1, :, None], axis=1))
    far_imag = lax.optimization_barrier(jnp.sum(adj_real * first_rows[:, 1, :, None] - adj_imag * first_rows[:, 0, :, None], axis=1))
    return (jnp.stack([own_real, own_imag], axis=1), jnp.stack([far_real, far_imag], axis=1))

def reference(spectra, observed, own_station, partner_station, pair_count):
    spec_rows = jnp.transpose(spectra, (2, 0, 1, 3))
    phase = phase_table(0, NF, 0, NT)
    cos_full = jnp.cos(phase) / math.sqrt(NF)
    sin_full = jnp.sin(phase) / math.sqrt(NF)
    basis = jnp.concatenate([cos_full.astype(jnp.bfloat16), -sin_full.astype(jnp.bfloat16)], axis=0)
    window = lag_window()
    slot_total = BLOCKS * CAP
    observed_blocks = observed.reshape(BLOCKS, slot_total * 9, NT)
    block_ids = jnp.repeat(jnp.arange(BLOCKS, dtype=jnp.int32), CAP)

    def one_reader(grad_all, inputs):
        reader, own_block, partner_block, count_row, observed_rows = inputs
        own_ids = reader * STA_DEV + own_block.reshape(slot_total)
        far_ids = block_ids * STA_DEV + partner_block.reshape(slot_total)
        alive_mask = (jnp.arange(CAP, dtype=jnp.int32)[None, :] < count_row[:, None]).reshape(slot_total).astype(jnp.float32)
        first_rows = spec_rows[own_ids].astype(jnp.float32)
        second_rows = spec_rows[far_ids].astype(jnp.float32)
        cross = (cross_spectra(first_rows, second_rows) * alive_mask[:, None, None, None, None]).astype(jnp.bfloat16)
        correlation = jnp.dot(cross.reshape(slot_total * 9, 2 * NF), basis, preferred_element_type=jnp.float32)
        residual = ((correlation - observed_rows.astype(jnp.float32)) * jnp.repeat(alive_mask, 9)[:, None] * window[None, :]).astype(jnp.bfloat16)
        adjoint_rows = lax.dot_general(residual, basis, (((1,), (1,)), ((), ())), preferred_element_type=jnp.float32).astype(jnp.bfloat16)
        own_grad, far_grad = pair_gradients(adjoint_rows.reshape(slot_total, 3, 3, 2, NF).astype(jnp.float32), first_rows, second_rows)
        grad_all = grad_all.at[own_ids].add(own_grad).at[far_ids].add(far_grad)
        return (grad_all, None)
    grad_start = jnp.zeros((STATIONS, 2, 3, NF), jnp.float32)
    readers = jnp.arange(BLOCKS, dtype=jnp.int32)
    grad_all, unused = lax.scan(one_reader, grad_start, (readers, own_station, partner_station, pair_count, observed_blocks))
    output_scale = 1.0 / math.sqrt(2.0 * BLOCKS * CAP / STA_DEV)
    real_term = jnp.einsum('sak,kt->tas', grad_all[:, 0], cos_full, precision=lax.Precision.HIGHEST)
    imag_term = jnp.einsum('sak,kt->tas', grad_all[:, 1], sin_full, precision=lax.Precision.HIGHEST)
    return (real_term - imag_term) * output_scale
```

```python
import functools
import math

import jax
import jax.numpy as jnp
import ml_dtypes
import numpy as np
from jax import lax
from jax.experimental import pallas as pl
from jax.experimental.pallas import tpu as pltpu
from jax.sharding import PartitionSpec as P

NF = 512
NT = 1024
LAG = NT // 4
MESH = pl.DeviceIdType.MESH
BF = jnp.bfloat16
F32 = jnp.float32


def tables():
    freq = np.arange(NF, dtype=np.int64)
    time = np.arange(NT, dtype=np.int64)
    num = (2 * freq + 1)[:, None] * time[None, :] % (2 * NT)
    phase = num.astype(np.float32) * np.float32(math.pi / NT)
    scale = np.float32(math.sqrt(NF))
    full = np.concatenate([np.cos(phase) / scale, -(np.sin(phase) / scale)], axis=0)
    high = full.astype(ml_dtypes.bfloat16)
    low = (full - high.astype(np.float32)).astype(ml_dtypes.bfloat16)
    kept = np.concatenate([high[:, :LAG], high[:, NT - LAG :]], axis=1)
    return high, low, np.ascontiguousarray(kept.T)


def loop(count, body):
    if count <= 8:
        for step in range(count):
            body(step)
    else:

        def wrapped(step, carry):
            body(step)
            return carry

        lax.fori_loop(0, count, wrapped, 0)


def kernel(
    n_b, n_q, cap, sta, item, scale,
    spec_ref, obs_ref, own_ref, part_ref, cnt_ref, high_ref, low_ref, kept_ref,
    out_ref,
    spec, obs, high, low, kept, obsf,
    g_send, g_recv, g_own, own_send, own_recv, row_send, row_recv,
    far_send, far_recv, ownt_send, ownt_recv,
    local_sem, g_ss, g_rs, own_ss, own_rs, row_ss, row_rs, far_ss, far_rs, ownt_ss, ownt_rs,
):
    per = n_b // n_q
    rows = cap * 8
    cols = 8 * sta
    band = NF // n_q
    half = NT // n_q // 2
    chunk = min(item, 16)
    chunks = item // chunk
    prow = -(-9 * chunk // 16) * 16
    blocks = chunk // cap
    b = lax.axis_index("blk")
    q = lax.axis_index("frq")
    home = lax.div(b, per)
    slot_in = lax.rem(b, per)

    loads = [
        pltpu.make_async_copy(spec_ref.at[0], spec.at[0, pl.ds(0, 3)], local_sem.at[0]),
        pltpu.make_async_copy(spec_ref.at[1], spec.at[1, pl.ds(0, 3)], local_sem.at[1]),
        pltpu.make_async_copy(obs_ref, obs, local_sem.at[2]),
        pltpu.make_async_copy(high_ref, high, local_sem.at[3]),
        pltpu.make_async_copy(kept_ref, kept, local_sem.at[4]),
        pltpu.make_async_copy(low_ref, low, local_sem.at[5]),
    ]
    for load in loads:
        load.start()

    barrier = pltpu.get_barrier_semaphore()
    total = n_b * n_q
    me = b * n_q + q

    def greet(step):
        other = lax.rem(me + 1 + step, total)
        pl.semaphore_signal(
            barrier, inc=1, device_id=(lax.div(other, n_q), lax.rem(other, n_q)), device_id_type=MESH
        )

    if total <= 32:
        for step in range(total - 1):
            greet(step)
    else:
        loop(total - 1, greet)

    row_i = lax.broadcasted_iota(jnp.int32, (rows, cols), 0)
    col_i = lax.broadcasted_iota(jnp.int32, (rows, cols), 1)
    row_s = lax.div(row_i, 8)
    base = col_i - lax.rem(row_i, 8) * sta

    def pick(ids, block):
        chosen = jnp.full((rows, cols), ids[0, block], jnp.int32)
        for s in range(1, cap):
            chosen = jnp.where(row_s == s, ids[s, block], chosen)
        return jnp.where(base == chosen, 1.0, 0.0).astype(BF)

    def build(block):
        g_send[block] = pick(part_ref, block)
        g_own[block] = pick(own_ref, block)

    loop(n_b, build)
    spec[0, 3] = jnp.zeros((sta, band), BF)
    spec[1, 3] = jnp.zeros((sta, band), BF)
    pl.semaphore_wait(barrier, total - 1)

    def g_copy(block, slot):
        return pltpu.make_async_remote_copy(
            src_ref=g_send.at[block], dst_ref=g_recv.at[slot], send_sem=g_ss.at[block],
            recv_sem=g_rs.at[slot], device_id=(block, q), device_id_type=MESH,
        )

    def g_start(step):
        block = lax.rem(b + 1 + step, n_b)
        g_copy(block, b).start()

    loop(n_b - 1, g_start)
    g_recv[b] = g_send[b]

    loads[0].wait()
    loads[1].wait()
    station_rows = spec[...].reshape(cols, band)

    def own_copy(peer, slot):
        return pltpu.make_async_remote_copy(
            src_ref=own_send.at[peer], dst_ref=own_recv.at[slot], send_sem=own_ss.at[peer],
            recv_sem=own_rs.at[slot], device_id=(b, peer), device_id_type=MESH,
        )

    picked = jnp.dot(
        g_own[...].reshape(n_b * rows, cols), station_rows, preferred_element_type=F32
    ).astype(BF)
    own_send[...] = picked.reshape(n_q, item * 8, band)
    for step in range(n_q - 1):
        own_copy(lax.rem(q + 1 + step, n_q), q).start()
    own_recv[q] = own_send[q]

    p_i = lax.broadcasted_iota(jnp.int32, (prow, 1), 0)
    p_ae = lax.div(p_i, chunk)
    p_slot = lax.rem(p_i, chunk)
    p_a = sum((p_ae >= 3 * m).astype(jnp.int32) for m in (1, 2, 3))
    p_e = jnp.where(p_ae >= 9, 3, p_ae - 3 * p_a)
    e_col = lax.broadcasted_iota(jnp.int32, (prow, chunk * 8), 1)

    def expand(component):
        want = p_slot * 8 + component
        return jnp.concatenate(
            [jnp.where(e_col == want + 4 * ri, 1.0, 0.0) for ri in range(2)], axis=0
        ).astype(BF)

    expand_u = expand(p_a)
    expand_v = expand(p_e)
    s_row = lax.broadcasted_iota(jnp.int32, (chunk * 8, prow), 0)
    s_col = lax.broadcasted_iota(jnp.int32, (chunk * 8, prow), 1)
    s_ae = lax.div(s_col, chunk)
    s_a = sum((s_ae >= 3 * m).astype(jnp.int32) for m in (1, 2, 3))
    s_e = jnp.where(s_ae >= 9, 3, s_ae - 3 * s_a)
    s_same = lax.div(s_row, 8) == lax.rem(s_col, chunk)
    s_comp = lax.rem(s_row, 4)
    sum_e = jnp.where(s_same & (s_a == s_comp), 1.0, 0.0).astype(BF)
    sum_a = jnp.where(s_same & (s_e == s_comp), 1.0, 0.0).astype(BF)
    lane = lax.broadcasted_iota(jnp.int32, (prow, 2 * LAG), 1)
    lag = jnp.where(lane < LAG, lane, 2 * LAG - lane)
    in_window = (lag >= NT // 32) & (lag < NT // 4)

    def prepare(at):
        if prow > 9 * chunk:
            obsf[9 * chunk :, :] = jnp.zeros((prow - 9 * chunk, 2 * LAG), F32)
        for a in range(3):
            for e in range(3):
                slab = obs[a, e, pl.ds(at * chunk, chunk), :] if chunks > 1 else obs[a, e]
                at_row = (3 * a + e) * chunk
                obsf[at_row : at_row + chunk, :LAG] = slab[:, :LAG].astype(F32)
                obsf[at_row : at_row + chunk, LAG:] = slab[:, NT - LAG :].astype(F32)

    loads[2].wait()
    if chunks == 1:
        prepare(0)

    def g_wait(step):
        g_copy(lax.rem(b + 1 + step, n_b), lax.rem(b + 1 + step, n_b)).wait_recv()

    loop(n_b - 1, g_wait)
    row_send[...] = jnp.dot(
        g_recv[...].reshape(n_b * rows, cols), station_rows, preferred_element_type=F32
    ).astype(BF).reshape(n_b, rows, band)

    def row_copy(block, slot):
        return pltpu.make_async_remote_copy(
            src_ref=row_send.at[block], dst_ref=row_recv.at[slot], send_sem=row_ss.at[block],
            recv_sem=row_rs.at[slot], device_id=(block, home), device_id_type=MESH,
        )

    mine = q * per + slot_in

    def row_start(step):
        row_copy(lax.rem(b + 1 + step, n_b), mine).start()

    loop(n_b - 1, row_start)

    @pl.when(q != home)
    def _():
        row_copy(b, mine).start()

    @pl.when(q == home)
    def _():
        row_recv[mine] = row_send[b]

    for step in range(n_q - 1):
        peer = lax.rem(q + 1 + step, n_q)
        own_copy(peer, peer).wait_recv()

    def row_wait(source):
        block = q * per + lax.rem(source, per)
        peer = lax.div(source, per)

        @pl.when(jnp.logical_or(block != b, peer != q))
        def _():
            row_copy(b, source).wait_recv()

    loop(n_q * per, lambda source: row_wait(jnp.int32(source)))
    loads[3].wait()
    loads[4].wait()
    loads[5].wait()

    def far_copy(peer, inner, slot):
        return pltpu.make_async_remote_copy(
            src_ref=far_send.at[peer * per + inner], dst_ref=far_recv.at[slot],
            send_sem=far_ss.at[peer * per + inner], recv_sem=far_rs.at[slot],
            device_id=(q * per + inner, peer), device_id_type=MESH,
        )

    def ownt_copy(peer, slot):
        return pltpu.make_async_remote_copy(
            src_ref=ownt_send.at[peer], dst_ref=ownt_recv.at[slot], send_sem=ownt_ss.at[peer],
            recv_sem=ownt_rs.at[slot], device_id=(b, peer), device_id_type=MESH,
        )

    def send_quarter(peer):
        def far_start(inner):
            other = jnp.logical_or(q * per + inner != b, q != peer)

            @pl.when(other)
            def _():
                far_copy(peer, inner, b).start()

            @pl.when(jnp.logical_not(other))
            def _():
                far_recv[b] = far_send[peer * per + inner]

        loop(per, far_start)

        @pl.when(q != peer)
        def _():
            ownt_copy(peer, q).start()

        @pl.when(q == peer)
        def _():
            ownt_recv[peer] = ownt_send[peer]

    def work(at):
        if chunks > 1:
            prepare(at)
        alive = jnp.zeros((prow, 1), jnp.int32)
        for i in range(chunk):
            count = cnt_ref[0, q * per + at * blocks + i // cap]
            live = jnp.clip(count - i % cap, 0, 1)
            alive = jnp.where(p_slot == i, live, alive)
        alive = jnp.where(p_ae < 9, alive, 0)
        alive_f = alive.astype(F32)

        def spread(matrix, parts):
            outs = [jnp.dot(matrix, part, preferred_element_type=F32) for part in parts]
            both = jnp.concatenate(outs, axis=1)
            return both[:prow], both[prow:]

        ur, ui = spread(
            expand_u,
            [own_recv[p, pl.ds(at * chunk * 8, chunk * 8), :] for p in range(n_q)],
        )
        vr, vi = spread(
            expand_v,
            [
                row_recv[pl.ds(p * per + at * blocks, blocks)].reshape(chunk * 8, band)
                for p in range(n_q)
            ],
        )
        cross = jnp.concatenate(
            [(ur * vr + ui * vi) * alive_f, (ui * vr - ur * vi) * alive_f], axis=1
        ).astype(BF)
        correlation = jnp.concatenate(
            [
                jnp.dot(cross, high[:, :LAG], preferred_element_type=F32),
                jnp.dot(cross, high[:, NT - LAG :], preferred_element_type=F32),
            ],
            axis=1,
        )
        residual = jnp.where(
            in_window & (alive > 0), correlation - obsf[...], 0.0
        ).astype(BF)
        adj = jnp.dot(residual, kept[...], preferred_element_type=F32).astype(BF).astype(F32)
        ar, ai = adj[:, :NF], adj[:, NF:]

        def reduce(matrix, real, imag):
            terms = jnp.concatenate([real, imag], axis=1)
            top = terms.astype(BF)
            rest = (terms - top.astype(F32)).astype(BF)
            return jnp.dot(matrix, top, preferred_element_type=F32) + jnp.dot(
                matrix, rest, preferred_element_type=F32
            )

        grad = jnp.concatenate(
            [
                reduce(sum_e, ar * vr - ai * vi, ar * vi + ai * vr),
                reduce(sum_a, ar * ur + ai * ui, ar * ui - ai * ur),
            ],
            axis=0,
        )
        top = grad.astype(BF)
        rest = (grad - top.astype(F32)).astype(BF)
        stacked = jnp.concatenate([top, rest], axis=0)
        count = chunk * 16
        first_half = lax.rem(lax.broadcasted_iota(jnp.int32, (count, half), 0), 8) < 4
        for peer in range(n_q):
            at_col = peer * 2 * half
            product = jnp.dot(
                stacked, high[:, at_col : at_col + 2 * half], preferred_element_type=F32
            )
            product = (
                product[:count]
                + product[count:]
                + jnp.dot(top, low[:, at_col : at_col + 2 * half], preferred_element_type=F32)
            ) * scale
            message = jnp.where(first_half, product[:, :half], product[:, half:])
            ownt_send[peer, pl.ds(at * chunk * 8, chunk * 8), :] = message[: chunk * 8]
            far_send[pl.ds(peer * per + at * blocks, blocks)] = (
                message[chunk * 8 :].astype(BF).reshape(blocks, rows, half)
            )
            if chunks == 1:
                send_quarter(peer)

    if chunks == 1:
        work(0)
    else:

        def work_step(at, carry):
            work(at)
            return carry

        lax.fori_loop(0, chunks, work_step, 0)
        for peer in range(n_q):
            send_quarter(peer)

    for step in range(n_q - 1):
        peer = lax.rem(q + 1 + step, n_q)
        ownt_copy(peer, peer).wait_recv()

    def far_wait(block):
        @pl.when(jnp.logical_or(block != b, q != home))
        def _():
            far_copy(0, 0, block).wait_recv()

    loop(n_b, lambda block: far_wait(jnp.int32(block)))

    def scatter(matrix, values):
        return lax.dot_general(
            matrix, values, (((0,), (0,)), ((), ())), preferred_element_type=F32
        )

    own_time = ownt_recv[...].reshape(n_q * item * 8, half)
    own_top = own_time.astype(BF)
    own_rest = (own_time - own_top.astype(F32)).astype(BF)
    g_mine = g_own[...].reshape(n_b * rows, cols)
    summed = (
        scatter(g_recv[...].reshape(n_b * rows, cols), far_recv[...].reshape(n_b * rows, half))
        + scatter(g_mine, own_top)
        + scatter(g_mine, own_rest)
    )
    for h in range(2):
        at_row = h * 4 * sta
        out_ref[:, :, h * half : (h + 1) * half] = summed[at_row : at_row + 3 * sta].reshape(
            3, sta, half
        )

    loop(n_b - 1, lambda step: g_copy(lax.rem(b + 1 + step, n_b), b).wait_send())
    loop(n_b - 1, lambda step: row_copy(lax.rem(b + 1 + step, n_b), mine).wait_send())

    @pl.when(q != home)
    def _():
        row_copy(b, mine).wait_send()

    for step in range(n_q - 1):
        peer = lax.rem(q + 1 + step, n_q)
        own_copy(peer, q).wait_send()
        ownt_copy(peer, q).wait_send()

    def far_done(index):
        peer = lax.div(index, per)
        inner = lax.rem(index, per)

        @pl.when(jnp.logical_or(q * per + inner != b, q != peer))
        def _():
            far_copy(peer, inner, b).wait_send()

    loop(n_q * per, lambda index: far_done(jnp.int32(index)))


def local(spectra, observed, own_station, partner_station, pair_count):
    n_b = lax.axis_size("blk")
    n_q = lax.axis_size("frq")
    sta = spectra.shape[2]
    band = spectra.shape[3]
    cap = own_station.shape[2]
    item = observed.shape[0]
    per = n_b // n_q
    rows = cap * 8
    cols = 8 * sta
    half = NT // n_q // 2
    chunk = min(item, 16)
    prow = -(-9 * chunk // 16) * 16
    scale = 1.0 / math.sqrt(2.0 * n_b * cap / sta)
    high, low, kept = tables()
    dma = pltpu.SemaphoreType.DMA
    anywhere = pl.BlockSpec(memory_space=pl.ANY)
    scalar = pl.BlockSpec(memory_space=pltpu.SMEM)
    out = pl.pallas_call(
        functools.partial(kernel, n_b, n_q, cap, sta, item, scale),
        out_shape=jax.ShapeDtypeStruct((3, sta, 2 * half), F32),
        in_specs=[anywhere, anywhere, scalar, scalar, scalar, anywhere, anywhere, anywhere],
        out_specs=pl.BlockSpec(memory_space=pltpu.VMEM),
        scratch_shapes=[
            pltpu.VMEM((2, 4, sta, band), BF),
            pltpu.VMEM((3, 3, item, NT), BF),
            pltpu.VMEM(high.shape, BF),
            pltpu.VMEM(low.shape, BF),
            pltpu.VMEM(kept.shape, BF),
            pltpu.VMEM((prow, 2 * LAG), F32),
            pltpu.VMEM((n_b, rows, cols), BF),
            pltpu.VMEM((n_b, rows, cols), BF),
            pltpu.VMEM((n_b, rows, cols), BF),
            pltpu.VMEM((n_q, item * 8, band), BF),
            pltpu.VMEM((n_q, item * 8, band), BF),
            pltpu.VMEM((n_b, rows, band), BF),
            pltpu.VMEM((n_q * per, rows, band), BF),
            pltpu.VMEM((n_q * per, rows, half), BF),
            pltpu.VMEM((n_b, rows, half), BF),
            pltpu.VMEM((n_q, item * 8, half), F32),
            pltpu.VMEM((n_q, item * 8, half), F32),
            dma((6,)),
            dma((n_b,)),
            dma((n_b,)),
            dma((n_q,)),
            dma((n_q,)),
            dma((n_b,)),
            dma((n_q * per,)),
            dma((n_q * per,)),
            dma((n_b,)),
            dma((n_q,)),
            dma((n_q,)),
        ],
        compiler_params=pltpu.CompilerParams(
            collective_id=0, has_side_effects=True, vmem_limit_bytes=48 * 1024 * 1024
        ),
        cost_estimate=pl.CostEstimate(flops=400_000_000, bytes_accessed=6_000_000, transcendentals=0),
    )(
        spectra,
        jnp.transpose(observed, (1, 2, 0, 3)),
        jnp.transpose(own_station[0], (1, 0)),
        jnp.transpose(partner_station[0], (1, 0)),
        pair_count,
        jnp.asarray(high),
        jnp.asarray(low),
        jnp.asarray(kept),
    )
    return jnp.transpose(out, (2, 0, 1))


def solution(mesh):
    return jax.shard_map(
        local,
        mesh=mesh,
        in_specs=(
            P(None, None, "blk", "frq"),
            P(("blk", "frq"), None, None, None),
            P("blk", None, None),
            P("blk", None, None),
            P("blk", None),
        ),
        out_specs=P("frq", None, "blk"),
        check_vma=False,
    )
```

```python
import functools
import math

import jax
import jax.numpy as jnp
import ml_dtypes
import numpy as np
from jax import lax
from jax.experimental import pallas as pl
from jax.experimental.pallas import tpu as pltpu
from jax.sharding import PartitionSpec as P

NF = 512
NT = 1024
LAG = NT // 4
MESH = pl.DeviceIdType.MESH
BF = jnp.bfloat16
F32 = jnp.float32


def tables():
    freq = np.arange(NF, dtype=np.int64)
    time = np.arange(NT, dtype=np.int64)
    num = (2 * freq + 1)[:, None] * time[None, :] % (2 * NT)
    phase = num.astype(np.float32) * np.float32(math.pi / NT)
    scale = np.float32(math.sqrt(NF))
    full = np.concatenate([np.cos(phase) / scale, -(np.sin(phase) / scale)], axis=0)
    high = full.astype(ml_dtypes.bfloat16)
    kept = np.concatenate([high[:, :LAG], high[:, NT - LAG :]], axis=1)
    return high, np.ascontiguousarray(kept.T)


def loop(count, body):
    if count <= 8:
        for step in range(count):
            body(step)
    else:

        def wrapped(step, carry):
            body(step)
            return carry

        lax.fori_loop(0, count, wrapped, 0)


def kernel(
    n_b, n_q, cap, sta, item, scale,
    spec_ref, obs_ref, own_in, part_in, cnt_in, high_ref, kept_ref,
    out_ref,
    own_ref, part_ref, cnt_ref, spec, obs, high, kept, obsf,
    g_send, g_recv, g_own, own_send, own_recv, row_send, row_recv,
    far_send, far_recv, ownt_send, ownt_recv,
    local_sem, g_ss, g_rs, own_ss, own_rs, row_ss, row_rs, far_ss, far_rs, ownt_ss, ownt_rs,
):
    per = n_b // n_q
    rows = cap * 8
    cols = 8 * sta
    band = NF // n_q
    half = NT // n_q // 2
    chunk = min(item, 16)
    chunks = item // chunk
    prow = -(-9 * chunk // 16) * 16
    blocks = chunk // cap
    b = lax.axis_index("blk")
    q = lax.axis_index("frq")
    home = lax.div(b, per)
    slot_in = lax.rem(b, per)

    id_loads = [
        pltpu.make_async_copy(part_in, part_ref, local_sem.at[5]),
        pltpu.make_async_copy(own_in, own_ref, local_sem.at[6]),
        pltpu.make_async_copy(cnt_in, cnt_ref, local_sem.at[7]),
    ]
    for load in id_loads:
        load.start()
    loads = [
        pltpu.make_async_copy(spec_ref.at[0], spec.at[0, pl.ds(0, 3)], local_sem.at[0]),
        pltpu.make_async_copy(spec_ref.at[1], spec.at[1, pl.ds(0, 3)], local_sem.at[1]),
        pltpu.make_async_copy(obs_ref, obs, local_sem.at[2]),
        pltpu.make_async_copy(high_ref, high, local_sem.at[3]),
        pltpu.make_async_copy(kept_ref, kept, local_sem.at[4]),
    ]
    for load in loads:
        load.start()

    barrier = pltpu.get_barrier_semaphore()

    def greet(step):
        pl.semaphore_signal(
            barrier, inc=1, device_id=(lax.rem(b + 1 + step, n_b), q), device_id_type=MESH
        )

    for step in range(n_q - 1):
        pl.semaphore_signal(
            barrier, inc=1, device_id=(b, lax.rem(q + 1 + step, n_q)), device_id_type=MESH
        )
    loop(n_b - 1, greet)

    row_i = lax.broadcasted_iota(jnp.int32, (rows, cols), 0)
    col_i = lax.broadcasted_iota(jnp.int32, (rows, cols), 1)
    row_s = lax.div(row_i, 8)
    base = col_i - lax.rem(row_i, 8) * sta

    def pick(ids, block):
        chosen = jnp.full((rows, cols), ids[0, block], jnp.int32)
        for s in range(1, cap):
            chosen = jnp.where(row_s == s, ids[s, block], chosen)
        return jnp.where(base == chosen, 1.0, 0.0).astype(BF)

    def build(block):
        g_send[block] = pick(part_ref, block)
        g_own[block] = pick(own_ref, block)

    for load in id_loads:
        load.wait()
    loop(n_b, build)
    spec[0, 3] = jnp.zeros((sta, band), BF)
    spec[1, 3] = jnp.zeros((sta, band), BF)
    pl.semaphore_wait(barrier, n_b + n_q - 2)

    def g_copy(block, slot):
        return pltpu.make_async_remote_copy(
            src_ref=g_send.at[block], dst_ref=g_recv.at[slot], send_sem=g_ss.at[block],
            recv_sem=g_rs.at[slot], device_id=(block, q), device_id_type=MESH,
        )

    def g_start(step):
        block = lax.rem(b + 1 + step, n_b)
        g_copy(block, b).start()

    loop(n_b - 1, g_start)
    g_recv[b] = g_send[b]

    loads[0].wait()
    loads[1].wait()
    station_rows = spec[...].reshape(cols, band)

    def own_copy(peer, slot):
        return pltpu.make_async_remote_copy(
            src_ref=own_send.at[peer], dst_ref=own_recv.at[slot], send_sem=own_ss.at[peer],
            recv_sem=own_rs.at[slot], device_id=(b, peer), device_id_type=MESH,
        )

    picked = jnp.dot(
        g_own[...].reshape(n_b * rows, cols), station_rows, preferred_element_type=F32
    ).astype(BF)
    own_send[...] = picked.reshape(n_q, item * 8, band)
    for step in range(n_q - 1):
        own_copy(lax.rem(q + 1 + step, n_q), q).start()
    own_recv[q] = own_send[q]

    p_i = lax.broadcasted_iota(jnp.int32, (prow, 1), 0)
    p_ae = lax.div(p_i, chunk)
    p_slot = lax.rem(p_i, chunk)
    p_a = sum((p_ae >= 3 * m).astype(jnp.int32) for m in (1, 2, 3))
    p_e = jnp.where(p_ae >= 9, 3, p_ae - 3 * p_a)
    e_col = lax.broadcasted_iota(jnp.int32, (prow, chunk * 8), 1)

    def expand(component):
        want = p_slot * 8 + component
        return jnp.concatenate(
            [jnp.where(e_col == want + 4 * ri, 1.0, 0.0) for ri in range(2)], axis=0
        ).astype(BF)

    expand_u = expand(p_a)
    expand_v = expand(p_e)
    s_row = lax.broadcasted_iota(jnp.int32, (chunk * 8, prow), 0)
    s_col = lax.broadcasted_iota(jnp.int32, (chunk * 8, prow), 1)
    s_ae = lax.div(s_col, chunk)
    s_a = sum((s_ae >= 3 * m).astype(jnp.int32) for m in (1, 2, 3))
    s_e = jnp.where(s_ae >= 9, 3, s_ae - 3 * s_a)
    s_same = lax.div(s_row, 8) == lax.rem(s_col, chunk)
    s_comp = lax.rem(s_row, 4)
    sum_e = jnp.where(s_same & (s_a == s_comp), 1.0, 0.0).astype(BF)
    sum_a = jnp.where(s_same & (s_e == s_comp), 1.0, 0.0).astype(BF)
    lane = lax.broadcasted_iota(jnp.int32, (prow, 2 * LAG), 1)
    lag = jnp.where(lane < LAG, lane, 2 * LAG - lane)
    in_window = (lag >= NT // 32) & (lag < NT // 4)

    def prepare(at):
        if prow > 9 * chunk:
            obsf[9 * chunk :, :] = jnp.zeros((prow - 9 * chunk, 2 * LAG), F32)
        for a in range(3):
            for e in range(3):
                slab = obs[a, e, pl.ds(at * chunk, chunk), :] if chunks > 1 else obs[a, e]
                at_row = (3 * a + e) * chunk
                obsf[at_row : at_row + chunk, :LAG] = slab[:, :LAG].astype(F32)
                obsf[at_row : at_row + chunk, LAG:] = slab[:, NT - LAG :].astype(F32)

    loads[2].wait()
    if chunks == 1:
        prepare(0)

    def g_wait(step):
        g_copy(lax.rem(b + 1 + step, n_b), lax.rem(b + 1 + step, n_b)).wait_recv()

    loop(n_b - 1, g_wait)
    row_send[...] = jnp.dot(
        g_recv[...].reshape(n_b * rows, cols), station_rows, preferred_element_type=F32
    ).astype(BF).reshape(n_b, rows, band)

    def row_copy(block, slot):
        return pltpu.make_async_remote_copy(
            src_ref=row_send.at[block], dst_ref=row_recv.at[slot], send_sem=row_ss.at[block],
            recv_sem=row_rs.at[slot], device_id=(block, home), device_id_type=MESH,
        )

    mine = q * per + slot_in

    def row_start(step):
        row_copy(lax.rem(b + 1 + step, n_b), mine).start()

    loop(n_b - 1, row_start)

    @pl.when(q != home)
    def _():
        row_copy(b, mine).start()

    @pl.when(q == home)
    def _():
        row_recv[mine] = row_send[b]

    for step in range(n_q - 1):
        peer = lax.rem(q + 1 + step, n_q)
        own_copy(peer, peer).wait_recv()

    def row_wait(source):
        block = q * per + lax.rem(source, per)
        peer = lax.div(source, per)

        @pl.when(jnp.logical_or(block != b, peer != q))
        def _():
            row_copy(b, source).wait_recv()

    loop(n_q * per, lambda source: row_wait(jnp.int32(source)))
    loads[3].wait()
    loads[4].wait()

    def far_copy(peer, inner, slot):
        return pltpu.make_async_remote_copy(
            src_ref=far_send.at[peer * per + inner], dst_ref=far_recv.at[slot],
            send_sem=far_ss.at[peer * per + inner], recv_sem=far_rs.at[slot],
            device_id=(q * per + inner, peer), device_id_type=MESH,
        )

    def ownt_copy(peer, slot):
        return pltpu.make_async_remote_copy(
            src_ref=ownt_send.at[peer], dst_ref=ownt_recv.at[slot], send_sem=ownt_ss.at[peer],
            recv_sem=ownt_rs.at[slot], device_id=(b, peer), device_id_type=MESH,
        )

    def send_quarter(peer):
        def far_start(inner):
            other = jnp.logical_or(q * per + inner != b, q != peer)

            @pl.when(other)
            def _():
                far_copy(peer, inner, b).start()

            @pl.when(jnp.logical_not(other))
            def _():
                far_recv[b] = far_send[peer * per + inner]

        loop(per, far_start)

        @pl.when(q != peer)
        def _():
            ownt_copy(peer, q).start()

        @pl.when(q == peer)
        def _():
            ownt_recv[peer] = ownt_send[peer]

    def work(at):
        if chunks > 1:
            prepare(at)
        alive = jnp.zeros((prow, 1), jnp.int32)
        for i in range(chunk):
            count = cnt_ref[0, q * per + at * blocks + i // cap]
            live = jnp.clip(count - i % cap, 0, 1)
            alive = jnp.where(p_slot == i, live, alive)
        alive = jnp.where(p_ae < 9, alive, 0)
        alive_f = alive.astype(F32)

        def spread(matrix, parts):
            outs = [jnp.dot(matrix, part, preferred_element_type=F32) for part in parts]
            both = jnp.concatenate(outs, axis=1)
            return both[:prow], both[prow:]

        ur, ui = spread(
            expand_u,
            [own_recv[p, pl.ds(at * chunk * 8, chunk * 8), :] for p in range(n_q)],
        )
        vr, vi = spread(
            expand_v,
            [
                row_recv[pl.ds(p * per + at * blocks, blocks)].reshape(chunk * 8, band)
                for p in range(n_q)
            ],
        )
        cross = jnp.concatenate(
            [(ur * vr + ui * vi) * alive_f, (ui * vr - ur * vi) * alive_f], axis=1
        ).astype(BF)
        correlation = jnp.concatenate(
            [
                jnp.dot(cross, high[:, :LAG], preferred_element_type=F32),
                jnp.dot(cross, high[:, NT - LAG :], preferred_element_type=F32),
            ],
            axis=1,
        )
        residual = jnp.where(
            in_window & (alive > 0), correlation - obsf[...], 0.0
        ).astype(BF)
        adj = jnp.dot(residual, kept[...], preferred_element_type=F32).astype(BF).astype(F32)
        ar, ai = adj[:, :NF], adj[:, NF:]

        def reduce(matrix, real, imag):
            terms = jnp.concatenate([real, imag], axis=1)
            top = terms.astype(BF)
            rest = (terms - top.astype(F32)).astype(BF)
            return jnp.dot(matrix, top, preferred_element_type=F32) + jnp.dot(
                matrix, rest, preferred_element_type=F32
            )

        grad = jnp.concatenate(
            [
                reduce(sum_e, ar * vr - ai * vi, ar * vi + ai * vr),
                reduce(sum_a, ar * ur + ai * ui, ar * ui - ai * ur),
            ],
            axis=0,
        )
        top = grad.astype(BF)
        rest = (grad - top.astype(F32)).astype(BF)
        stacked = jnp.concatenate([top, rest], axis=0)
        count = chunk * 16
        first_half = lax.rem(lax.broadcasted_iota(jnp.int32, (count, half), 0), 8) < 4
        for peer in range(n_q):
            at_col = peer * 2 * half
            product = jnp.dot(
                stacked, high[:, at_col : at_col + 2 * half], preferred_element_type=F32
            )
            product = (product[:count] + product[count:]) * scale
            message = jnp.where(first_half, product[:, :half], product[:, half:])
            ownt_send[peer, pl.ds(at * chunk * 8, chunk * 8), :] = message[: chunk * 8]
            far_send[pl.ds(peer * per + at * blocks, blocks)] = (
                message[chunk * 8 :].astype(BF).reshape(blocks, rows, half)
            )
            if chunks == 1:
                send_quarter(peer)

    if chunks == 1:
        work(0)
    else:

        def work_step(at, carry):
            work(at)
            return carry

        lax.fori_loop(0, chunks, work_step, 0)
        for peer in range(n_q):
            send_quarter(peer)

    for step in range(n_q - 1):
        peer = lax.rem(q + 1 + step, n_q)
        ownt_copy(peer, peer).wait_recv()

    def far_wait(block):
        @pl.when(jnp.logical_or(block != b, q != home))
        def _():
            far_copy(0, 0, block).wait_recv()

    loop(n_b, lambda block: far_wait(jnp.int32(block)))

    def scatter(matrix, values):
        return lax.dot_general(
            matrix, values, (((0,), (0,)), ((), ())), preferred_element_type=F32
        )

    own_time = ownt_recv[...].reshape(n_q * item * 8, half)
    own_top = own_time.astype(BF)
    own_rest = (own_time - own_top.astype(F32)).astype(BF)
    g_mine = g_own[...].reshape(n_b * rows, cols)
    summed = (
        scatter(g_recv[...].reshape(n_b * rows, cols), far_recv[...].reshape(n_b * rows, half))
        + scatter(g_mine, own_top)
        + scatter(g_mine, own_rest)
    )
    for h in range(2):
        at_row = h * 4 * sta
        out_ref[:, :, h * half : (h + 1) * half] = summed[at_row : at_row + 3 * sta].reshape(
            3, sta, half
        )

    loop(n_b - 1, lambda step: g_copy(lax.rem(b + 1 + step, n_b), b).wait_send())
    loop(n_b - 1, lambda step: row_copy(lax.rem(b + 1 + step, n_b), mine).wait_send())

    @pl.when(q != home)
    def _():
        row_copy(b, mine).wait_send()

    for step in range(n_q - 1):
        peer = lax.rem(q + 1 + step, n_q)
        own_copy(peer, q).wait_send()
        ownt_copy(peer, q).wait_send()

    def far_done(index):
        peer = lax.div(index, per)
        inner = lax.rem(index, per)

        @pl.when(jnp.logical_or(q * per + inner != b, q != peer))
        def _():
            far_copy(peer, inner, b).wait_send()

    loop(n_q * per, lambda index: far_done(jnp.int32(index)))


def local(spectra, observed, own_station, partner_station, pair_count):
    n_b = lax.axis_size("blk")
    n_q = lax.axis_size("frq")
    sta = spectra.shape[2]
    band = spectra.shape[3]
    cap = own_station.shape[2]
    item = observed.shape[0]
    per = n_b // n_q
    rows = cap * 8
    cols = 8 * sta
    half = NT // n_q // 2
    chunk = min(item, 16)
    prow = -(-9 * chunk // 16) * 16
    scale = 1.0 / math.sqrt(2.0 * n_b * cap / sta)
    high, kept = tables()
    dma = pltpu.SemaphoreType.DMA
    held = pl.BlockSpec(memory_space=pltpu.HBM)
    out = pl.pallas_call(
        functools.partial(kernel, n_b, n_q, cap, sta, item, scale),
        out_shape=jax.ShapeDtypeStruct((3, sta, 2 * half), F32),
        in_specs=[held] * 7,
        out_specs=pl.BlockSpec(memory_space=pltpu.VMEM),
        scratch_shapes=[
            pltpu.SMEM((cap, n_b), jnp.int32),
            pltpu.SMEM((cap, n_b), jnp.int32),
            pltpu.SMEM((1, n_b), jnp.int32),
            pltpu.VMEM((2, 4, sta, band), BF),
            pltpu.VMEM((3, 3, item, NT), BF),
            pltpu.VMEM(high.shape, BF),
            pltpu.VMEM(kept.shape, BF),
            pltpu.VMEM((prow, 2 * LAG), F32),
            pltpu.VMEM((n_b, rows, cols), BF),
            pltpu.VMEM((n_b, rows, cols), BF),
            pltpu.VMEM((n_b, rows, cols), BF),
            pltpu.VMEM((n_q, item * 8, band), BF),
            pltpu.VMEM((n_q, item * 8, band), BF),
            pltpu.VMEM((n_b, rows, band), BF),
            pltpu.VMEM((n_q * per, rows, band), BF),
            pltpu.VMEM((n_q * per, rows, half), BF),
            pltpu.VMEM((n_b, rows, half), BF),
            pltpu.VMEM((n_q, item * 8, half), F32),
            pltpu.VMEM((n_q, item * 8, half), F32),
            dma((8,)),
            dma((n_b,)),
            dma((n_b,)),
            dma((n_q,)),
            dma((n_q,)),
            dma((n_b,)),
            dma((n_q * per,)),
            dma((n_q * per,)),
            dma((n_b,)),
            dma((n_q,)),
            dma((n_q,)),
        ],
        compiler_params=pltpu.CompilerParams(
            collective_id=0, has_side_effects=True, vmem_limit_bytes=(64 * 1024 - 64) * 1024
        ),
        cost_estimate=pl.CostEstimate(flops=400_000_000, bytes_accessed=6_000_000, transcendentals=0),
    )(
        spectra,
        jnp.transpose(observed, (1, 2, 0, 3)),
        jnp.transpose(own_station[0], (1, 0)),
        jnp.transpose(partner_station[0], (1, 0)),
        pair_count,
        jnp.asarray(high),
        jnp.asarray(kept),
    )
    return jnp.transpose(out, (2, 0, 1))


def solution(mesh):
    return jax.shard_map(
        local,
        mesh=mesh,
        in_specs=(
            P(None, None, "blk", "frq"),
            P(("blk", "frq"), None, None, None),
            P("blk", None, None),
            P("blk", None, None),
            P("blk", None),
        ),
        out_specs=P("frq", None, "blk"),
        check_vma=False,
    )
```

```python
import functools
import math

import jax
import jax.numpy as jnp
import ml_dtypes
import numpy as np
from jax import lax
from jax.experimental import pallas as pl
from jax.experimental.pallas import tpu as pltpu
from jax.sharding import PartitionSpec as P

NF = 512
NT = 1024
LAG = NT // 4
MESH = pl.DeviceIdType.MESH
BF = jnp.bfloat16
F32 = jnp.float32


def tables():
    freq = np.arange(NF, dtype=np.int64)
    time = np.arange(NT, dtype=np.int64)
    num = (2 * freq + 1)[:, None] * time[None, :] % (2 * NT)
    phase = num.astype(np.float32) * np.float32(math.pi / NT)
    scale = np.float32(math.sqrt(NF))
    full = np.concatenate([np.cos(phase) / scale, -(np.sin(phase) / scale)], axis=0)
    high = full.astype(ml_dtypes.bfloat16)
    kept = np.concatenate([high[:, :LAG], high[:, NT - LAG :]], axis=1)
    return high, np.ascontiguousarray(kept.T)


def loop(count, body):
    if count <= 8:
        for step in range(count):
            body(step)
    else:

        def wrapped(step, carry):
            body(step)
            return carry

        lax.fori_loop(0, count, wrapped, 0)


def kernel(
    n_b, n_q, cap, sta, item, scale,
    spec_ref, obs_ref, own_in, part_in, cnt_in, high_ref, kept_ref,
    out_ref,
    own_ref, part_ref, cnt_ref, spec, obs, high, kept, obsf,
    g_send, g_recv, g_own, own_send, own_recv, row_send, row_recv,
    far_send, far_recv, ownt_send, ownt_recv,
    local_sem, g_ss, g_rs, own_ss, own_rs, row_ss, row_rs, far_ss, far_rs, ownt_ss, ownt_rs,
):
    per = n_b // n_q
    rows = cap * 8
    cols = 8 * sta
    band = NF // n_q
    half = NT // n_q // 2
    chunk = min(item, 16)
    chunks = item // chunk
    prow = -(-9 * chunk // 16) * 16
    blocks = chunk // cap
    bits = chunk.bit_length() - 1
    b = lax.axis_index("blk")
    q = lax.axis_index("frq")
    home = lax.div(b, per)
    slot_in = lax.rem(b, per)

    def wrap(value, size):
        return jnp.where(value >= size, value - size, value)

    id_loads = [
        pltpu.make_async_copy(part_in, part_ref, local_sem.at[5]),
        pltpu.make_async_copy(own_in, own_ref, local_sem.at[6]),
        pltpu.make_async_copy(cnt_in, cnt_ref, local_sem.at[7]),
    ]
    for load in id_loads:
        load.start()
    loads = [
        pltpu.make_async_copy(spec_ref.at[0], spec.at[0, pl.ds(0, 3)], local_sem.at[0]),
        pltpu.make_async_copy(spec_ref.at[1], spec.at[1, pl.ds(0, 3)], local_sem.at[1]),
        pltpu.make_async_copy(obs_ref, obs, local_sem.at[2]),
        pltpu.make_async_copy(
            high_ref.at[pl.ds(0, NF)], high.at[pl.ds(0, NF)], local_sem.at[3]
        ),
        pltpu.make_async_copy(
            high_ref.at[pl.ds(NF, NF)], high.at[pl.ds(NF, NF)], local_sem.at[4]
        ),
        pltpu.make_async_copy(kept_ref, kept, local_sem.at[8]),
    ]
    for load in loads[:3]:
        load.start()

    barrier = pltpu.get_barrier_semaphore()

    def greet(step):
        pl.semaphore_signal(
            barrier, inc=1, device_id=(wrap(b + 1 + step, n_b), q), device_id_type=MESH
        )

    for step in range(n_q - 1):
        pl.semaphore_signal(
            barrier, inc=1, device_id=(b, wrap(q + 1 + step, n_q)), device_id_type=MESH
        )
    loop(n_b - 1, greet)

    row_i = lax.broadcasted_iota(jnp.int32, (rows, cols), 0)
    col_i = lax.broadcasted_iota(jnp.int32, (rows, cols), 1)
    row_s = row_i >> 3
    base = col_i - (row_i & 7) * sta

    def pick(ids, block):
        chosen = jnp.full((rows, cols), ids[0, block], jnp.int32)
        for s in range(1, cap):
            chosen = jnp.where(row_s == s, ids[s, block], chosen)
        return jnp.where(base == chosen, 1.0, 0.0).astype(BF)

    def build(block):
        g_send[block] = pick(part_ref, block)
        g_own[block] = pick(own_ref, block)

    for load in id_loads:
        load.wait()
    loop(n_b, build)
    spec[0, 3] = jnp.zeros((sta, band), BF)
    spec[1, 3] = jnp.zeros((sta, band), BF)
    pl.semaphore_wait(barrier, n_b + n_q - 2)

    def many(src, dst, count, send_sem, recv_sem):
        return pltpu.make_async_remote_copy(
            src_ref=src.at[pl.ds(0, count)], dst_ref=dst.at[pl.ds(0, count)], send_sem=send_sem,
            recv_sem=recv_sem, device_id=(wrap(b + 1, n_b), q), device_id_type=MESH,
        )

    def wait_block(copy_of, wait):
        @pl.when(q == home)
        def _():
            wait(copy_of(n_b - 1))

        @pl.when(q != home)
        def _():
            wait(copy_of(n_b))

    def g_copy(block, slot):
        return pltpu.make_async_remote_copy(
            src_ref=g_send.at[block], dst_ref=g_recv.at[slot], send_sem=g_ss,
            recv_sem=g_rs, device_id=(block, q), device_id_type=MESH,
        )

    def g_start(step):
        block = wrap(b + 1 + step, n_b)
        g_copy(block, b).start()

    loop(n_b - 1, g_start)
    g_recv[b] = g_send[b]

    loads[0].wait()
    loads[1].wait()
    station_rows = spec[...].reshape(cols, band)

    def own_copy(peer, slot):
        return pltpu.make_async_remote_copy(
            src_ref=own_send.at[peer], dst_ref=own_recv.at[slot], send_sem=own_ss,
            recv_sem=own_rs, device_id=(b, peer), device_id_type=MESH,
        )

    picked = jnp.dot(
        g_own[...].reshape(n_b * rows, cols), station_rows, preferred_element_type=F32
    ).astype(BF)
    own_send[...] = picked.reshape(n_q, item * 8, band)
    for step in range(n_q - 1):
        own_copy(wrap(q + 1 + step, n_q), q).start()
    own_recv[q] = own_send[q]
    for load in loads[3:]:
        load.start()

    p_i = lax.broadcasted_iota(jnp.int32, (prow, 1), 0)
    p_ae = p_i >> bits
    p_slot = p_i & (chunk - 1)
    p_a = sum((p_ae >= 3 * m).astype(jnp.int32) for m in (1, 2, 3))
    p_e = jnp.where(p_ae >= 9, 3, p_ae - 3 * p_a)
    e_col = lax.broadcasted_iota(jnp.int32, (prow, chunk * 8), 1)

    def expand(component):
        want = p_slot * 8 + component
        return jnp.concatenate(
            [jnp.where(e_col == want + 4 * ri, 1.0, 0.0) for ri in range(2)], axis=0
        ).astype(BF)

    expand_u = expand(p_a)
    expand_v = expand(p_e)
    s_row = lax.broadcasted_iota(jnp.int32, (chunk * 8, prow), 0)
    s_col = lax.broadcasted_iota(jnp.int32, (chunk * 8, prow), 1)
    s_ae = s_col >> bits
    s_a = sum((s_ae >= 3 * m).astype(jnp.int32) for m in (1, 2, 3))
    s_e = jnp.where(s_ae >= 9, 3, s_ae - 3 * s_a)
    s_same = (s_row >> 3) == (s_col & (chunk - 1))
    s_comp = s_row & 3
    sum_e = jnp.where(s_same & (s_a == s_comp), 1.0, 0.0).astype(BF)
    sum_a = jnp.where(s_same & (s_e == s_comp), 1.0, 0.0).astype(BF)
    lane = lax.broadcasted_iota(jnp.int32, (prow, 2 * LAG), 1)
    lag = jnp.where(lane < LAG, lane, 2 * LAG - lane)
    in_window = (lag >= NT // 32) & (lag < NT // 4)

    def prepare(at):
        if prow > 9 * chunk:
            obsf[9 * chunk :, :] = jnp.zeros((prow - 9 * chunk, 2 * LAG), F32)
        for a in range(3):
            for e in range(3):
                slab = obs[a, e, pl.ds(at * chunk, chunk), :] if chunks > 1 else obs[a, e]
                at_row = (3 * a + e) * chunk
                obsf[at_row : at_row + chunk, :LAG] = slab[:, :LAG].astype(F32)
                obsf[at_row : at_row + chunk, LAG:] = slab[:, NT - LAG :].astype(F32)

    loads[2].wait()
    if chunks == 1:
        prepare(0)

    many(g_send, g_recv, n_b - 1, g_ss, g_rs).wait_recv()
    row_send[...] = jnp.dot(
        g_recv[...].reshape(n_b * rows, cols), station_rows, preferred_element_type=F32
    ).astype(BF).reshape(n_b, rows, band)

    def row_copy(block, slot):
        return pltpu.make_async_remote_copy(
            src_ref=row_send.at[block], dst_ref=row_recv.at[slot], send_sem=row_ss,
            recv_sem=row_rs, device_id=(block, home), device_id_type=MESH,
        )

    mine = q * per + slot_in

    def row_start(step):
        row_copy(wrap(b + 1 + step, n_b), mine).start()

    loop(n_b - 1, row_start)

    @pl.when(q != home)
    def _():
        row_copy(b, mine).start()

    @pl.when(q == home)
    def _():
        row_recv[mine] = row_send[b]

    many(own_send, own_recv, n_q - 1, own_ss, own_rs).wait_recv()

    def spread(matrix, parts):
        outs = [jnp.dot(matrix, part, preferred_element_type=F32) for part in parts]
        both = jnp.concatenate(outs, axis=1)
        return both[:prow], both[prow:]

    def spread_own(at):
        return spread(
            expand_u,
            [own_recv[p, pl.ds(at * chunk * 8, chunk * 8), :] for p in range(n_q)],
        )

    early = spread_own(0) if chunks == 1 else None
    wait_block(
        lambda count: many(row_send, row_recv, count, row_ss, row_rs), lambda c: c.wait_recv()
    )
    for load in loads[3:]:
        load.wait()

    def far_copy(peer, inner, slot):
        return pltpu.make_async_remote_copy(
            src_ref=far_send.at[peer * per + inner], dst_ref=far_recv.at[slot],
            send_sem=far_ss, recv_sem=far_rs,
            device_id=(q * per + inner, peer), device_id_type=MESH,
        )

    def ownt_copy(peer, slot):
        return pltpu.make_async_remote_copy(
            src_ref=ownt_send.at[peer], dst_ref=ownt_recv.at[slot], send_sem=ownt_ss,
            recv_sem=ownt_rs, device_id=(b, peer), device_id_type=MESH,
        )

    def send_quarter(peer):
        def far_start(inner):
            other = jnp.logical_or(q * per + inner != b, q != peer)

            @pl.when(other)
            def _():
                far_copy(peer, inner, b).start()

            @pl.when(jnp.logical_not(other))
            def _():
                far_recv[b] = far_send[peer * per + inner]

        loop(per, far_start)

        @pl.when(q != peer)
        def _():
            ownt_copy(peer, q).start()

        @pl.when(q == peer)
        def _():
            ownt_recv[peer] = ownt_send[peer]

    def work(at):
        if chunks > 1:
            prepare(at)
        alive = jnp.zeros((prow, 1), jnp.int32)
        for i in range(chunk):
            count = cnt_ref[0, q * per + at * blocks + i // cap]
            live = jnp.clip(count - i % cap, 0, 1)
            alive = jnp.where(p_slot == i, live, alive)
        alive = jnp.where(p_ae < 9, alive, 0)
        alive_f = alive.astype(F32)

        ur, ui = early if chunks == 1 else spread_own(at)
        vr, vi = spread(
            expand_v,
            [
                row_recv[pl.ds(p * per + at * blocks, blocks)].reshape(chunk * 8, band)
                for p in range(n_q)
            ],
        )
        cross = jnp.concatenate(
            [(ur * vr + ui * vi) * alive_f, (ui * vr - ur * vi) * alive_f], axis=1
        ).astype(BF)
        correlation = jnp.concatenate(
            [
                jnp.dot(cross, high[:, :LAG], preferred_element_type=F32),
                jnp.dot(cross, high[:, NT - LAG :], preferred_element_type=F32),
            ],
            axis=1,
        )
        residual = jnp.where(
            in_window & (alive > 0), correlation - obsf[...], 0.0
        ).astype(BF)
        adj = jnp.dot(residual, kept[...], preferred_element_type=F32).astype(BF).astype(F32)
        ar, ai = adj[:, :NF], adj[:, NF:]

        def reduce(matrix, real, imag):
            terms = jnp.concatenate([real, imag], axis=1)
            top = terms.astype(BF)
            rest = (terms - top.astype(F32)).astype(BF)
            return jnp.dot(matrix, top, preferred_element_type=F32) + jnp.dot(
                matrix, rest, preferred_element_type=F32
            )

        grad = jnp.concatenate(
            [
                reduce(sum_e, ar * vr - ai * vi, ar * vi + ai * vr),
                reduce(sum_a, ar * ur + ai * ui, ar * ui - ai * ur),
            ],
            axis=0,
        )
        top = grad.astype(BF)
        rest = (grad - top.astype(F32)).astype(BF)
        stacked = jnp.concatenate([top, rest], axis=0)
        count = chunk * 16
        first_half = (lax.broadcasted_iota(jnp.int32, (count, half), 0) & 7) < 4
        for peer in range(n_q):
            at_col = peer * 2 * half
            product = jnp.dot(
                stacked, high[:, at_col : at_col + 2 * half], preferred_element_type=F32
            )
            product = (product[:count] + product[count:]) * scale
            message = jnp.where(first_half, product[:, :half], product[:, half:])
            ownt_send[peer, pl.ds(at * chunk * 8, chunk * 8), :] = message[: chunk * 8]
            far_send[pl.ds(peer * per + at * blocks, blocks)] = (
                message[chunk * 8 :].astype(BF).reshape(blocks, rows, half)
            )
            if chunks == 1:
                send_quarter(peer)

    if chunks == 1:
        work(0)
    else:

        def work_step(at, carry):
            work(at)
            return carry

        lax.fori_loop(0, chunks, work_step, 0)
        for peer in range(n_q):
            send_quarter(peer)

    def scatter(matrix, values):
        return lax.dot_general(
            matrix, values, (((0,), (0,)), ((), ())), preferred_element_type=F32
        )

    many(ownt_send, ownt_recv, n_q - 1, ownt_ss, ownt_rs).wait_recv()
    own_time = ownt_recv[...].reshape(n_q * item * 8, half)
    own_top = own_time.astype(BF)
    own_rest = (own_time - own_top.astype(F32)).astype(BF)
    g_mine = g_own[...].reshape(n_b * rows, cols)
    own_sum = scatter(g_mine, own_top) + scatter(g_mine, own_rest)
    wait_block(
        lambda count: many(far_send, far_recv, count, far_ss, far_rs), lambda c: c.wait_recv()
    )
    summed = own_sum + scatter(
        g_recv[...].reshape(n_b * rows, cols), far_recv[...].reshape(n_b * rows, half)
    )
    for h in range(2):
        at_row = h * 4 * sta
        out_ref[:, :, h * half : (h + 1) * half] = summed[at_row : at_row + 3 * sta].reshape(
            3, sta, half
        )

    many(g_send, g_recv, n_b - 1, g_ss, g_rs).wait_send()
    many(own_send, own_recv, n_q - 1, own_ss, own_rs).wait_send()
    many(ownt_send, ownt_recv, n_q - 1, ownt_ss, ownt_rs).wait_send()
    wait_block(
        lambda count: many(row_send, row_recv, count, row_ss, row_rs), lambda c: c.wait_send()
    )
    wait_block(
        lambda count: many(far_send, far_recv, count, far_ss, far_rs), lambda c: c.wait_send()
    )


def local(spectra, observed, own_station, partner_station, pair_count):
    n_b = lax.axis_size("blk")
    n_q = lax.axis_size("frq")
    sta = spectra.shape[2]
    band = spectra.shape[3]
    cap = own_station.shape[2]
    item = observed.shape[0]
    per = n_b // n_q
    rows = cap * 8
    cols = 8 * sta
    half = NT // n_q // 2
    chunk = min(item, 16)
    prow = -(-9 * chunk // 16) * 16
    scale = 1.0 / math.sqrt(2.0 * n_b * cap / sta)
    high, kept = tables()
    dma = pltpu.SemaphoreType.DMA
    held = pl.BlockSpec(memory_space=pltpu.HBM)
    out = pl.pallas_call(
        functools.partial(kernel, n_b, n_q, cap, sta, item, scale),
        out_shape=jax.ShapeDtypeStruct((3, sta, 2 * half), F32),
        in_specs=[held] * 7,
        out_specs=pl.BlockSpec(memory_space=pltpu.VMEM),
        scratch_shapes=[
            pltpu.SMEM((cap, n_b), jnp.int32),
            pltpu.SMEM((cap, n_b), jnp.int32),
            pltpu.SMEM((1, n_b), jnp.int32),
            pltpu.VMEM((2, 4, sta, band), BF),
            pltpu.VMEM((3, 3, item, NT), BF),
            pltpu.VMEM(high.shape, BF),
            pltpu.VMEM(kept.shape, BF),
            pltpu.VMEM((prow, 2 * LAG), F32),
            pltpu.VMEM((n_b, rows, cols), BF),
            pltpu.VMEM((n_b, rows, cols), BF),
            pltpu.VMEM((n_b, rows, cols), BF),
            pltpu.VMEM((n_q, item * 8, band), BF),
            pltpu.VMEM((n_q, item * 8, band), BF),
            pltpu.VMEM((n_b, rows, band), BF),
            pltpu.VMEM((n_q * per, rows, band), BF),
            pltpu.VMEM((n_q * per, rows, half), BF),
            pltpu.VMEM((n_b, rows, half), BF),
            pltpu.VMEM((n_q, item * 8, half), F32),
            pltpu.VMEM((n_q, item * 8, half), F32),
            dma((9,)),
            *[dma(())] * 10,
        ],
        compiler_params=pltpu.CompilerParams(
            collective_id=0, has_side_effects=True, vmem_limit_bytes=32 * 1024 * 1024
        ),
        cost_estimate=pl.CostEstimate(flops=400_000_000, bytes_accessed=6_000_000, transcendentals=0),
    )(
        *(
            pltpu.with_memory_space_constraint(operand, pltpu.HBM)
            for operand in (
                spectra,
                jnp.transpose(observed, (1, 2, 0, 3)),
                jnp.transpose(own_station[0], (1, 0)),
                jnp.transpose(partner_station[0], (1, 0)),
                pair_count,
                jnp.asarray(high),
                jnp.asarray(kept),
            )
        )
    )
    return jnp.transpose(out, (2, 0, 1))


def solution(mesh):
    return jax.shard_map(
        local,
        mesh=mesh,
        in_specs=(
            P(None, None, "blk", "frq"),
            P(("blk", "frq"), None, None, None),
            P("blk", None, None),
            P("blk", None, None),
            P("blk", None),
        ),
        out_specs=P("frq", None, "blk"),
        check_vma=False,
    )
```

```python
import functools
import math

import jax
import jax.numpy as jnp
import ml_dtypes
import numpy as np
from jax import lax
from jax.experimental import pallas as pl
from jax.experimental.pallas import tpu as pltpu
from jax.sharding import PartitionSpec as P

NF = 512
NT = 1024
LAG = NT // 4
MESH = pl.DeviceIdType.MESH
BF = jnp.bfloat16
F32 = jnp.float32


def tables():
    freq = np.arange(NF, dtype=np.int64)
    time = np.arange(NT, dtype=np.int64)
    num = (2 * freq + 1)[:, None] * time[None, :] % (2 * NT)
    phase = num.astype(np.float32) * np.float32(math.pi / NT)
    scale = np.float32(math.sqrt(NF))
    full = np.concatenate([np.cos(phase) / scale, -(np.sin(phase) / scale)], axis=0)
    high = full.astype(ml_dtypes.bfloat16)
    kept = np.concatenate([high[:, :LAG], high[:, NT - LAG :]], axis=1)
    return high, np.ascontiguousarray(kept.T)


def loop(count, body):
    if count <= 8:
        for step in range(count):
            body(step)
    else:

        def wrapped(step, carry):
            body(step)
            return carry

        lax.fori_loop(0, count, wrapped, 0)


def kernel(
    n_b, n_q, cap, sta, item, scale,
    spec_ref, obs_ref, own_in, part_in, cnt_in, high_ref, kept_ref,
    out_ref,
    own_ref, part_ref, cnt_ref, spec, obs, high, kept, obsf,
    g_send, g_recv, g_own, g_turn, own_send, own_recv, row_send, row_recv,
    far_send, far_recv, ownt_send, ownt_recv,
    local_sem, g_ss, g_rs, own_ss, own_rs, row_ss, row_rs, far_ss, far_rs, ownt_ss, ownt_rs,
):
    per = n_b // n_q
    rows = cap * 8
    cols = 8 * sta
    band = NF // n_q
    half = NT // n_q // 2
    chunk = min(item, 16)
    chunks = item // chunk
    prow = -(-9 * chunk // 16) * 16
    blocks = chunk // cap
    bits = chunk.bit_length() - 1
    b = lax.axis_index("blk")
    q = lax.axis_index("frq")
    home = lax.div(b, per)
    slot_in = lax.rem(b, per)

    def wrap(value, size):
        return jnp.where(value >= size, value - size, value)

    id_loads = [
        pltpu.make_async_copy(part_in, part_ref, local_sem.at[5]),
        pltpu.make_async_copy(own_in, own_ref, local_sem.at[6]),
        pltpu.make_async_copy(cnt_in, cnt_ref, local_sem.at[7]),
    ]
    for load in id_loads:
        load.start()
    loads = [
        pltpu.make_async_copy(spec_ref.at[0], spec.at[0, pl.ds(0, 3)], local_sem.at[0]),
        pltpu.make_async_copy(spec_ref.at[1], spec.at[1, pl.ds(0, 3)], local_sem.at[1]),
        pltpu.make_async_copy(obs_ref, obs, local_sem.at[2]),
        pltpu.make_async_copy(
            high_ref.at[pl.ds(0, NF)], high.at[pl.ds(0, NF)], local_sem.at[3]
        ),
        pltpu.make_async_copy(
            high_ref.at[pl.ds(NF, NF)], high.at[pl.ds(NF, NF)], local_sem.at[4]
        ),
        pltpu.make_async_copy(kept_ref, kept, local_sem.at[8]),
    ]
    barrier = pltpu.get_barrier_semaphore()

    def greet(step):
        pl.semaphore_signal(
            barrier, inc=1, device_id=(wrap(b + 1 + step, n_b), q), device_id_type=MESH
        )

    for step in range(n_q - 1):
        pl.semaphore_signal(
            barrier, inc=1, device_id=(b, wrap(q + 1 + step, n_q)), device_id_type=MESH
        )
    loop(n_b - 1, greet)
    for load in loads:
        load.start()

    row_i = lax.broadcasted_iota(jnp.int32, (rows, cols), 0)
    col_i = lax.broadcasted_iota(jnp.int32, (rows, cols), 1)
    row_s = row_i >> 3
    base = col_i - (row_i & 7) * sta

    def pick(ids, block):
        chosen = jnp.full((rows, cols), ids[0, block], jnp.int32)
        for s in range(1, cap):
            chosen = jnp.where(row_s == s, ids[s, block], chosen)
        return jnp.where(base == chosen, 1.0, 0.0).astype(BF)

    def build(block):
        g_send[block] = pick(part_ref, block)

    def build_own(block):
        g_own[block] = pick(own_ref, block)

    for load in id_loads:
        load.wait()
    loop(n_b, build)
    pl.semaphore_wait(barrier, n_b + n_q - 2)

    def many(src, dst, count, send_sem, recv_sem):
        return pltpu.make_async_remote_copy(
            src_ref=src.at[pl.ds(0, count)], dst_ref=dst.at[pl.ds(0, count)], send_sem=send_sem,
            recv_sem=recv_sem, device_id=(wrap(b + 1, n_b), q), device_id_type=MESH,
        )

    def wait_block(copy_of, wait):
        @pl.when(q == home)
        def _():
            wait(copy_of(n_b - 1))

        @pl.when(q != home)
        def _():
            wait(copy_of(n_b))

    def g_copy(block, slot):
        return pltpu.make_async_remote_copy(
            src_ref=g_send.at[block], dst_ref=g_recv.at[slot], send_sem=g_ss,
            recv_sem=g_rs, device_id=(block, q), device_id_type=MESH,
        )

    def g_start(step):
        block = wrap(b + 1 + step, n_b)
        g_copy(block, b).start()

    loop(n_b - 1, g_start)
    g_recv[b] = g_send[b]

    loop(n_b, build_own)
    spec[0, 3] = jnp.zeros((sta, band), BF)
    spec[1, 3] = jnp.zeros((sta, band), BF)
    loads[0].wait()
    loads[1].wait()
    station_rows = spec[...].reshape(cols, band)

    def own_copy(peer, slot):
        return pltpu.make_async_remote_copy(
            src_ref=own_send.at[peer], dst_ref=own_recv.at[slot], send_sem=own_ss,
            recv_sem=own_rs, device_id=(b, peer), device_id_type=MESH,
        )

    picked = jnp.dot(
        g_own[...].reshape(n_b * rows, cols), station_rows, preferred_element_type=F32
    ).astype(BF)
    own_send[...] = picked.reshape(n_q, item * 8, band)
    for step in range(n_q - 1):
        own_copy(wrap(q + 1 + step, n_q), q).start()
    own_recv[q] = own_send[q]

    p_i = lax.broadcasted_iota(jnp.int32, (prow, 1), 0)
    p_ae = p_i >> bits
    p_slot = p_i & (chunk - 1)
    p_a = sum((p_ae >= 3 * m).astype(jnp.int32) for m in (1, 2, 3))
    p_e = jnp.where(p_ae >= 9, 3, p_ae - 3 * p_a)
    e_col = lax.broadcasted_iota(jnp.int32, (prow, chunk * 8), 1)

    def expand(component):
        want = p_slot * 8 + component
        return jnp.concatenate(
            [jnp.where(e_col == want + 4 * ri, 1.0, 0.0) for ri in range(2)], axis=0
        ).astype(BF)

    expand_u = expand(p_a)
    expand_v = expand(p_e)
    s_row = lax.broadcasted_iota(jnp.int32, (chunk * 8, prow), 0)
    s_col = lax.broadcasted_iota(jnp.int32, (chunk * 8, prow), 1)
    s_ae = s_col >> bits
    s_a = sum((s_ae >= 3 * m).astype(jnp.int32) for m in (1, 2, 3))
    s_e = jnp.where(s_ae >= 9, 3, s_ae - 3 * s_a)
    s_same = (s_row >> 3) == (s_col & (chunk - 1))
    s_comp = s_row & 3
    sum_e = jnp.where(s_same & (s_a == s_comp), 1.0, 0.0)
    sum_a = jnp.where(s_same & (s_e == s_comp), 1.0, 0.0)
    none = jnp.zeros((chunk * 8, prow), F32)
    sums = jnp.concatenate(
        [
            jnp.concatenate([sum_e, sum_e, none, none], axis=1),
            jnp.concatenate([none, none, sum_a, sum_a], axis=1),
        ],
        axis=0,
    ).astype(BF)
    lane = lax.broadcasted_iota(jnp.int32, (prow, 2 * LAG), 1)
    lag = jnp.where(lane < LAG, lane, 2 * LAG - lane)
    in_window = (lag >= NT // 32) & (lag < NT // 4)

    def prepare(at):
        if prow > 9 * chunk:
            obsf[9 * chunk :, :] = jnp.zeros((prow - 9 * chunk, 2 * LAG), F32)
        for a in range(3):
            for e in range(3):
                slab = obs[a, e, pl.ds(at * chunk, chunk), :] if chunks > 1 else obs[a, e]
                at_row = (3 * a + e) * chunk
                obsf[at_row : at_row + chunk, :LAG] = slab[:, :LAG].astype(F32)
                obsf[at_row : at_row + chunk, LAG:] = slab[:, NT - LAG :].astype(F32)

    loads[2].wait()
    if chunks == 1:
        prepare(0)

    many(g_send, g_recv, n_b - 1, g_ss, g_rs).wait_recv()
    row_send[...] = jnp.dot(
        g_recv[...].reshape(n_b * rows, cols), station_rows, preferred_element_type=F32
    ).astype(BF).reshape(n_b, rows, band)

    def row_copy(block, slot):
        return pltpu.make_async_remote_copy(
            src_ref=row_send.at[block], dst_ref=row_recv.at[slot], send_sem=row_ss,
            recv_sem=row_rs, device_id=(block, home), device_id_type=MESH,
        )

    mine = q * per + slot_in

    def row_start(step):
        row_copy(wrap(b + 1 + step, n_b), mine).start()

    loop(n_b - 1, row_start)

    @pl.when(q != home)
    def _():
        row_copy(b, mine).start()

    @pl.when(q == home)
    def _():
        row_recv[mine] = row_send[b]

    turn_i = lax.broadcasted_iota(jnp.int32, (cols, cols), 0)
    turn_j = lax.broadcasted_iota(jnp.int32, (cols, cols), 1)
    eye = jnp.where(turn_i == turn_j, 1.0, 0.0).astype(BF)

    def turned(matrix):
        return lax.dot_general(
            eye, matrix[...].reshape(n_b * rows, cols), (((1,), (1,)), ((), ())),
            preferred_element_type=F32,
        ).astype(BF)

    g_turn[0] = turned(g_recv)
    g_turn[1] = turned(g_own)
    many(own_send, own_recv, n_q - 1, own_ss, own_rs).wait_recv()

    def spread(matrix, parts):
        both = jnp.dot(matrix, jnp.concatenate(parts, axis=1), preferred_element_type=F32)
        return both[:prow], both[prow:]

    def spread_own(at):
        return spread(
            expand_u,
            [own_recv[p, pl.ds(at * chunk * 8, chunk * 8), :] for p in range(n_q)],
        )

    def first_part(at):
        alive = jnp.zeros((prow, 1), jnp.int32)
        for i in range(chunk):
            count = cnt_ref[0, q * per + at * blocks + i // cap]
            live = jnp.clip(count - i % cap, 0, 1)
            alive = jnp.where(p_slot == i, live, alive)
        alive = jnp.where(p_ae < 9, alive, 0)
        alive_f = alive.astype(F32)
        keep = in_window & (alive > 0)
        ur, ui = spread_own(at)
        return ur, ui, alive_f, keep

    early = first_part(0) if chunks == 1 else None
    wait_block(
        lambda count: many(row_send, row_recv, count, row_ss, row_rs), lambda c: c.wait_recv()
    )
    for load in loads[3:]:
        load.wait()

    def far_copy(peer, inner, slot):
        return pltpu.make_async_remote_copy(
            src_ref=far_send.at[peer * per + inner], dst_ref=far_recv.at[slot],
            send_sem=far_ss, recv_sem=far_rs,
            device_id=(q * per + inner, peer), device_id_type=MESH,
        )

    def ownt_copy(peer, slot):
        return pltpu.make_async_remote_copy(
            src_ref=ownt_send.at[peer], dst_ref=ownt_recv.at[slot], send_sem=ownt_ss,
            recv_sem=ownt_rs, device_id=(b, peer), device_id_type=MESH,
        )

    def send_quarter(peer):
        def far_start(inner):
            other = jnp.logical_or(q * per + inner != b, q != peer)

            @pl.when(other)
            def _():
                far_copy(peer, inner, b).start()

            @pl.when(jnp.logical_not(other))
            def _():
                far_recv[b] = far_send[peer * per + inner]

        loop(per, far_start)

        @pl.when(q != peer)
        def _():
            ownt_copy(peer, q).start()

        @pl.when(q == peer)
        def _():
            ownt_recv[peer] = ownt_send[peer]

    def work(at):
        if chunks > 1:
            prepare(at)
        ur, ui, alive_f, keep = early if chunks == 1 else first_part(at)
        vr, vi = spread(
            expand_v,
            [
                row_recv[pl.ds(p * per + at * blocks, blocks)].reshape(chunk * 8, band)
                for p in range(n_q)
            ],
        )
        cross = jnp.concatenate(
            [(ur * vr + ui * vi) * alive_f, (ui * vr - ur * vi) * alive_f], axis=1
        ).astype(BF)
        correlation = jnp.concatenate(
            [
                jnp.dot(cross, high[:, :LAG], preferred_element_type=F32),
                jnp.dot(cross, high[:, NT - LAG :], preferred_element_type=F32),
            ],
            axis=1,
        )
        residual = jnp.where(keep, correlation - obsf[...], 0.0).astype(BF)
        adj = jnp.dot(residual, kept[...], preferred_element_type=F32).astype(BF).astype(F32)
        ar, ai = adj[:, :NF], adj[:, NF:]

        def halves(real, imag):
            terms = jnp.concatenate([real, imag], axis=1)
            upper = terms.astype(BF)
            return [upper, (terms - upper.astype(F32)).astype(BF)]

        terms = jnp.concatenate(
            halves(ar * vr - ai * vi, ar * vi + ai * vr)
            + halves(ar * ur + ai * ui, ar * ui - ai * ur),
            axis=0,
        )
        grad = jnp.dot(sums, terms, preferred_element_type=F32)
        top = grad.astype(BF)
        rest = (grad - top.astype(F32)).astype(BF)
        stacked = jnp.concatenate([top, rest], axis=0)
        count = chunk * 16
        first_half = (lax.broadcasted_iota(jnp.int32, (count, half), 0) & 7) < 4
        for peer in range(n_q):
            at_col = peer * 2 * half
            product = jnp.dot(
                stacked, high[:, at_col : at_col + 2 * half], preferred_element_type=F32
            )
            product = (product[:count] + product[count:]) * scale
            message = jnp.where(first_half, product[:, :half], product[:, half:])
            ownt_send[peer, pl.ds(at * chunk * 8, chunk * 8), :] = message[: chunk * 8]
            far_send[pl.ds(peer * per + at * blocks, blocks)] = (
                message[chunk * 8 :].astype(BF).reshape(blocks, rows, half)
            )
            if chunks == 1:
                send_quarter(peer)

    if chunks == 1:
        work(0)
    else:

        def work_step(at, carry):
            work(at)
            return carry

        lax.fori_loop(0, chunks, work_step, 0)
        for peer in range(n_q):
            send_quarter(peer)

    def scatter(matrix, values):
        return jnp.dot(matrix, values, preferred_element_type=F32)

    many(ownt_send, ownt_recv, n_q - 1, ownt_ss, ownt_rs).wait_recv()
    own_time = ownt_recv[...].reshape(n_q * item * 8, half)
    own_top = own_time.astype(BF)
    own_rest = (own_time - own_top.astype(F32)).astype(BF)
    own_sum = scatter(g_turn[1], own_top) + scatter(g_turn[1], own_rest)
    wait_block(
        lambda count: many(far_send, far_recv, count, far_ss, far_rs), lambda c: c.wait_recv()
    )
    summed = own_sum + scatter(g_turn[0], far_recv[...].reshape(n_b * rows, half))
    for h in range(2):
        at_row = h * 4 * sta
        out_ref[:, :, h * half : (h + 1) * half] = summed[at_row : at_row + 3 * sta].reshape(
            3, sta, half
        )

    many(g_send, g_recv, n_b - 1, g_ss, g_rs).wait_send()
    many(own_send, own_recv, n_q - 1, own_ss, own_rs).wait_send()
    many(ownt_send, ownt_recv, n_q - 1, ownt_ss, ownt_rs).wait_send()
    wait_block(
        lambda count: many(row_send, row_recv, count, row_ss, row_rs), lambda c: c.wait_send()
    )
    wait_block(
        lambda count: many(far_send, far_recv, count, far_ss, far_rs), lambda c: c.wait_send()
    )


def local(spectra, observed, own_station, partner_station, pair_count):
    n_b = lax.axis_size("blk")
    n_q = lax.axis_size("frq")
    sta = spectra.shape[2]
    band = spectra.shape[3]
    cap = own_station.shape[2]
    item = observed.shape[0]
    per = n_b // n_q
    rows = cap * 8
    cols = 8 * sta
    half = NT // n_q // 2
    chunk = min(item, 16)
    prow = -(-9 * chunk // 16) * 16
    scale = 1.0 / math.sqrt(2.0 * n_b * cap / sta)
    high, kept = tables()
    dma = pltpu.SemaphoreType.DMA
    held = pl.BlockSpec(memory_space=pltpu.HBM)
    out = pl.pallas_call(
        functools.partial(kernel, n_b, n_q, cap, sta, item, scale),
        out_shape=jax.ShapeDtypeStruct((3, sta, 2 * half), F32),
        in_specs=[held] * 7,
        out_specs=pl.BlockSpec(memory_space=pltpu.VMEM),
        scratch_shapes=[
            pltpu.SMEM((cap, n_b), jnp.int32),
            pltpu.SMEM((cap, n_b), jnp.int32),
            pltpu.SMEM((1, n_b), jnp.int32),
            pltpu.VMEM((2, 4, sta, band), BF),
            pltpu.VMEM((3, 3, item, NT), BF),
            pltpu.VMEM(high.shape, BF),
            pltpu.VMEM(kept.shape, BF),
            pltpu.VMEM((prow, 2 * LAG), F32),
            pltpu.VMEM((n_b, rows, cols), BF),
            pltpu.VMEM((n_b, rows, cols), BF),
            pltpu.VMEM((n_b, rows, cols), BF),
            pltpu.VMEM((2, cols, n_b * rows), BF),
            pltpu.VMEM((n_q, item * 8, band), BF),
            pltpu.VMEM((n_q, item * 8, band), BF),
            pltpu.VMEM((n_b, rows, band), BF),
            pltpu.VMEM((n_q * per, rows, band), BF),
            pltpu.VMEM((n_q * per, rows, half), BF),
            pltpu.VMEM((n_b, rows, half), BF),
            pltpu.VMEM((n_q, item * 8, half), F32),
            pltpu.VMEM((n_q, item * 8, half), F32),
            dma((9,)),
            *[dma(())] * 10,
        ],
        compiler_params=pltpu.CompilerParams(
            collective_id=0, has_side_effects=True, vmem_limit_bytes=32 * 1024 * 1024
        ),
        cost_estimate=pl.CostEstimate(flops=400_000_000, bytes_accessed=6_000_000, transcendentals=0),
    )(
        *(
            pltpu.with_memory_space_constraint(operand, pltpu.HBM)
            for operand in (
                spectra,
                jnp.transpose(observed, (1, 2, 0, 3)),
                jnp.transpose(own_station[0], (1, 0)),
                jnp.transpose(partner_station[0], (1, 0)),
                pair_count,
                jnp.asarray(high),
                jnp.asarray(kept),
            )
        )
    )
    return jnp.transpose(out, (2, 0, 1))


def solution(mesh):
    return jax.shard_map(
        local,
        mesh=mesh,
        in_specs=(
            P(None, None, "blk", "frq"),
            P(("blk", "frq"), None, None, None),
            P("blk", None, None),
            P("blk", None, None),
            P("blk", None),
        ),
        out_specs=P("frq", None, "blk"),
        check_vma=False,
    )
```

```python
import functools
import math

import jax
import jax.numpy as jnp
import ml_dtypes
import numpy as np
from jax import lax
from jax.experimental import pallas as pl
from jax.experimental.pallas import tpu as pltpu
from jax.sharding import PartitionSpec as P

NF = 512
NT = 1024
LAG = NT // 4
MESH = pl.DeviceIdType.MESH
BF = jnp.bfloat16
F32 = jnp.float32


def tables():
    freq = np.arange(NF, dtype=np.int64)
    time = np.arange(NT, dtype=np.int64)
    num = (2 * freq + 1)[:, None] * time[None, :] % (2 * NT)
    phase = num.astype(np.float32) * np.float32(math.pi / NT)
    scale = np.float32(math.sqrt(NF))
    full = np.concatenate([np.cos(phase) / scale, -(np.sin(phase) / scale)], axis=0)
    high = full.astype(ml_dtypes.bfloat16)
    kept = np.concatenate([high[:, :LAG], high[:, NT - LAG :]], axis=1)
    return high, np.ascontiguousarray(kept.T)


def loop(count, body):
    if count <= 2:
        for step in range(count):
            body(step)
    else:

        def wrapped(step, carry):
            body(step)
            return carry

        lax.fori_loop(0, count, wrapped, 0)


def tiles(count, body):
    def wrapped(step, carry):
        body(step)
        return carry

    lax.fori_loop(0, count, wrapped, 0)


def kernel(
    n_b, n_q, cap, sta, item, scale,
    spec_ref, obs_ref, own_in, part_in, cnt_in, high_ref, kept_ref,
    out_ref,
    own_ref, part_ref, cnt_ref, spec, obs, high, kept, obsf, corr, adjs,
    g_send, g_recv, g_own, g_turn, own_send, own_recv, row_send, row_recv,
    far_send, far_recv, ownt_send, ownt_recv,
    local_sem, g_ss, g_rs, own_ss, own_rs, row_ss, row_rs, far_ss, far_rs, ownt_ss, ownt_rs,
):
    per = n_b // n_q
    rows = cap * 8
    cols = 8 * sta
    band = NF // n_q
    half = NT // n_q // 2
    chunk = min(item, 16)
    chunks = item // chunk
    prow = -(-9 * chunk // 16) * 16
    blocks = chunk // cap
    bits = chunk.bit_length() - 1
    b = lax.axis_index("blk")
    q = lax.axis_index("frq")
    home = lax.div(b, per)
    slot_in = lax.rem(b, per)

    def wrap(value, size):
        return jnp.where(value >= size, value - size, value)

    id_loads = [
        pltpu.make_async_copy(part_in, part_ref, local_sem.at[5]),
        pltpu.make_async_copy(own_in, own_ref, local_sem.at[6]),
        pltpu.make_async_copy(cnt_in, cnt_ref, local_sem.at[7]),
    ]
    for load in id_loads:
        load.start()
    loads = [
        pltpu.make_async_copy(spec_ref.at[0], spec.at[0, pl.ds(0, 3)], local_sem.at[0]),
        pltpu.make_async_copy(spec_ref.at[1], spec.at[1, pl.ds(0, 3)], local_sem.at[1]),
        pltpu.make_async_copy(obs_ref, obs, local_sem.at[2]),
        pltpu.make_async_copy(
            high_ref.at[pl.ds(0, NF)], high.at[pl.ds(0, NF)], local_sem.at[3]
        ),
        pltpu.make_async_copy(
            high_ref.at[pl.ds(NF, NF)], high.at[pl.ds(NF, NF)], local_sem.at[4]
        ),
        pltpu.make_async_copy(kept_ref, kept, local_sem.at[8]),
    ]
    barrier = pltpu.get_barrier_semaphore()

    def greet(step):
        pl.semaphore_signal(
            barrier, inc=1, device_id=(wrap(b + 1 + step, n_b), q), device_id_type=MESH
        )

    def greet_band(step):
        pl.semaphore_signal(
            barrier, inc=1, device_id=(b, wrap(q + 1 + step, n_q)), device_id_type=MESH
        )

    loop(n_q - 1, greet_band)
    loop(n_b - 1, greet)
    for load in loads:
        load.start()

    row_i = lax.broadcasted_iota(jnp.int32, (rows, cols), 0)
    col_i = lax.broadcasted_iota(jnp.int32, (rows, cols), 1)
    row_s = row_i >> 3
    base = col_i - (row_i & 7) * sta

    def pick(ids, block):
        chosen = jnp.full((rows, cols), ids[0, block], jnp.int32)
        for s in range(1, cap):
            chosen = jnp.where(row_s == s, ids[s, block], chosen)
        return jnp.where(base == chosen, 1.0, 0.0).astype(BF)

    def build(block):
        g_send[block] = pick(part_ref, block)

    def build_own(block):
        g_own[block] = pick(own_ref, block)

    for load in id_loads:
        load.wait()
    loop(n_b, build)
    pl.semaphore_wait(barrier, n_b + n_q - 2)

    def many(src, dst, count, send_sem, recv_sem):
        return pltpu.make_async_remote_copy(
            src_ref=src.at[pl.ds(0, count)], dst_ref=dst.at[pl.ds(0, count)], send_sem=send_sem,
            recv_sem=recv_sem, device_id=(wrap(b + 1, n_b), q), device_id_type=MESH,
        )

    def wait_block(copy_of, wait):
        @pl.when(q == home)
        def _():
            wait(copy_of(n_b - 1))

        @pl.when(q != home)
        def _():
            wait(copy_of(n_b))

    def g_copy(block, slot):
        return pltpu.make_async_remote_copy(
            src_ref=g_send.at[block], dst_ref=g_recv.at[slot], send_sem=g_ss,
            recv_sem=g_rs, device_id=(block, q), device_id_type=MESH,
        )

    def g_start(step):
        block = wrap(b + 1 + step, n_b)
        g_copy(block, b).start()

    loop(n_b - 1, g_start)
    g_recv[b] = g_send[b]

    loop(n_b, build_own)
    spec[0, 3] = jnp.zeros((sta, band), BF)
    spec[1, 3] = jnp.zeros((sta, band), BF)
    loads[0].wait()
    loads[1].wait()
    station_rows = spec[...].reshape(cols, band)

    def own_copy(peer, slot):
        return pltpu.make_async_remote_copy(
            src_ref=own_send.at[peer], dst_ref=own_recv.at[slot], send_sem=own_ss,
            recv_sem=own_rs, device_id=(b, peer), device_id_type=MESH,
        )

    picked = jnp.dot(
        g_own[...].reshape(n_b * rows, cols), station_rows, preferred_element_type=F32
    ).astype(BF)
    own_send[...] = picked.reshape(n_q, item * 8, band)
    loop(n_q - 1, lambda step: own_copy(wrap(q + 1 + step, n_q), q).start())
    own_recv[q] = own_send[q]

    p_i = lax.broadcasted_iota(jnp.int32, (prow, 1), 0)
    p_ae = p_i >> bits
    p_slot = p_i & (chunk - 1)
    p_a = sum((p_ae >= 3 * m).astype(jnp.int32) for m in (1, 2, 3))
    p_e = jnp.where(p_ae >= 9, 3, p_ae - 3 * p_a)
    e_col = lax.broadcasted_iota(jnp.int32, (prow, chunk * 8), 1)

    def expand(component):
        want = p_slot * 8 + component
        return jnp.concatenate(
            [jnp.where(e_col == want + 4 * ri, 1.0, 0.0) for ri in range(2)], axis=0
        ).astype(BF)

    expand_u = expand(p_a)
    expand_v = expand(p_e)
    s_row = lax.broadcasted_iota(jnp.int32, (chunk * 8, prow), 0)
    s_col = lax.broadcasted_iota(jnp.int32, (chunk * 8, prow), 1)
    s_ae = s_col >> bits
    s_a = sum((s_ae >= 3 * m).astype(jnp.int32) for m in (1, 2, 3))
    s_e = jnp.where(s_ae >= 9, 3, s_ae - 3 * s_a)
    s_same = (s_row >> 3) == (s_col & (chunk - 1))
    s_comp = s_row & 3
    sum_e = jnp.where(s_same & (s_a == s_comp), 1.0, 0.0)
    sum_a = jnp.where(s_same & (s_e == s_comp), 1.0, 0.0)
    none = jnp.zeros((chunk * 8, prow), F32)
    sums = jnp.concatenate(
        [
            jnp.concatenate([sum_e, sum_e, none, none], axis=1),
            jnp.concatenate([none, none, sum_a, sum_a], axis=1),
        ],
        axis=0,
    ).astype(BF)
    lane = lax.broadcasted_iota(jnp.int32, (prow, 2 * LAG), 1)
    lag = jnp.where(lane < LAG, lane, 2 * LAG - lane)
    in_window = (lag >= NT // 32) & (lag < NT // 4)

    def prepare(at):
        if prow > 9 * chunk:
            obsf[9 * chunk :, :] = jnp.zeros((prow - 9 * chunk, 2 * LAG), F32)
        for a in range(3):
            for e in range(3):
                slab = obs[a, e, pl.ds(at * chunk, chunk), :] if chunks > 1 else obs[a, e]
                at_row = (3 * a + e) * chunk
                obsf[at_row : at_row + chunk, :LAG] = slab[:, :LAG].astype(F32)
                obsf[at_row : at_row + chunk, LAG:] = slab[:, NT - LAG :].astype(F32)

    loads[2].wait()
    if chunks == 1:
        prepare(0)

    many(g_send, g_recv, n_b - 1, g_ss, g_rs).wait_recv()
    row_send[...] = jnp.dot(
        g_recv[...].reshape(n_b * rows, cols), station_rows, preferred_element_type=F32
    ).astype(BF).reshape(n_b, rows, band)

    def row_copy(block, slot):
        return pltpu.make_async_remote_copy(
            src_ref=row_send.at[block], dst_ref=row_recv.at[slot], send_sem=row_ss,
            recv_sem=row_rs, device_id=(block, home), device_id_type=MESH,
        )

    mine = q * per + slot_in

    def row_start(step):
        row_copy(wrap(b + 1 + step, n_b), mine).start()

    loop(n_b - 1, row_start)

    @pl.when(q != home)
    def _():
        row_copy(b, mine).start()

    @pl.when(q == home)
    def _():
        row_recv[mine] = row_send[b]

    turn_i = lax.broadcasted_iota(jnp.int32, (cols, cols), 0)
    turn_j = lax.broadcasted_iota(jnp.int32, (cols, cols), 1)
    eye = jnp.where(turn_i == turn_j, 1.0, 0.0).astype(BF)

    def turned(matrix):
        return lax.dot_general(
            eye, matrix[...].reshape(n_b * rows, cols), (((1,), (1,)), ((), ())),
            preferred_element_type=F32,
        ).astype(BF)

    g_turn[0] = turned(g_recv)
    g_turn[1] = turned(g_own)
    many(own_send, own_recv, n_q - 1, own_ss, own_rs).wait_recv()

    def spread(matrix, parts):
        both = jnp.dot(matrix, jnp.concatenate(parts, axis=1), preferred_element_type=F32)
        return both[:prow], both[prow:]

    def spread_own(at):
        return spread(
            expand_u,
            [own_recv[p, pl.ds(at * chunk * 8, chunk * 8), :] for p in range(n_q)],
        )

    def first_part(at):
        alive = jnp.zeros((prow, 1), jnp.int32)
        for i in range(chunk):
            count = cnt_ref[0, q * per + at * blocks + i // cap]
            live = jnp.clip(count - i % cap, 0, 1)
            alive = jnp.where(p_slot == i, live, alive)
        alive = jnp.where(p_ae < 9, alive, 0)
        alive_f = alive.astype(F32)
        keep = in_window & (alive > 0)
        ur, ui = spread_own(at)
        return ur, ui, alive_f, keep

    early = first_part(0) if chunks == 1 else None
    wait_block(
        lambda count: many(row_send, row_recv, count, row_ss, row_rs), lambda c: c.wait_recv()
    )
    for load in loads[3:]:
        load.wait()

    def far_copy(peer, inner, slot):
        return pltpu.make_async_remote_copy(
            src_ref=far_send.at[peer * per + inner], dst_ref=far_recv.at[slot],
            send_sem=far_ss, recv_sem=far_rs,
            device_id=(q * per + inner, peer), device_id_type=MESH,
        )

    def ownt_copy(peer, slot):
        return pltpu.make_async_remote_copy(
            src_ref=ownt_send.at[peer], dst_ref=ownt_recv.at[slot], send_sem=ownt_ss,
            recv_sem=ownt_rs, device_id=(b, peer), device_id_type=MESH,
        )

    def send_quarter(peer):
        def far_start(inner):
            other = jnp.logical_or(q * per + inner != b, q != peer)

            @pl.when(other)
            def _():
                far_copy(peer, inner, b).start()

            @pl.when(jnp.logical_not(other))
            def _():
                far_recv[b] = far_send[peer * per + inner]

        loop(per, far_start)

        @pl.when(q != peer)
        def _():
            ownt_copy(peer, q).start()

        @pl.when(q == peer)
        def _():
            ownt_recv[peer] = ownt_send[peer]

    def work(at):
        if chunks > 1:
            prepare(at)
        ur, ui, alive_f, keep = early if chunks == 1 else first_part(at)
        vr, vi = spread(
            expand_v,
            [
                row_recv[pl.ds(p * per + at * blocks, blocks)].reshape(chunk * 8, band)
                for p in range(n_q)
            ],
        )
        cross = jnp.concatenate(
            [(ur * vr + ui * vi) * alive_f, (ui * vr - ur * vi) * alive_f], axis=1
        ).astype(BF)

        def correlate(side):
            column = pl.ds(pl.multiple_of(side * (NT - LAG), LAG), LAG)
            into = pl.ds(pl.multiple_of(side * LAG, LAG), LAG)
            corr[:, into] = jnp.dot(cross, high[:, column], preferred_element_type=F32)

        tiles(2, correlate)
        residual = jnp.where(keep, corr[...] - obsf[...], 0.0).astype(BF)

        def back(tile):
            column = pl.ds(pl.multiple_of(tile * LAG, LAG), LAG)
            adjs[:, column] = jnp.dot(residual, kept[:, column], preferred_element_type=F32)

        tiles(2 * NF // LAG, back)
        adj = adjs[...].astype(BF).astype(F32)
        ar, ai = adj[:, :NF], adj[:, NF:]

        def halves(real, imag):
            terms = jnp.concatenate([real, imag], axis=1)
            upper = terms.astype(BF)
            return [upper, (terms - upper.astype(F32)).astype(BF)]

        terms = jnp.concatenate(
            halves(ar * vr - ai * vi, ar * vi + ai * vr)
            + halves(ar * ur + ai * ui, ar * ui - ai * ur),
            axis=0,
        )
        grad = jnp.dot(sums, terms, preferred_element_type=F32)
        top = grad.astype(BF)
        rest = (grad - top.astype(F32)).astype(BF)
        stacked = jnp.concatenate([top, rest], axis=0)
        count = chunk * 16
        first_half = (lax.broadcasted_iota(jnp.int32, (count, half), 0) & 7) < 4

        def quarter(peer):
            column = pl.ds(pl.multiple_of(peer * 2 * half, 2 * half), 2 * half)
            product = jnp.dot(stacked, high[:, column], preferred_element_type=F32)
            product = (product[:count] + product[count:]) * scale
            message = jnp.where(first_half, product[:, :half], product[:, half:])
            ownt_send[peer, pl.ds(at * chunk * 8, chunk * 8), :] = message[: chunk * 8]
            far_send[pl.ds(peer * per + at * blocks, blocks)] = (
                message[chunk * 8 :].astype(BF).reshape(blocks, rows, half)
            )
            if chunks == 1:
                send_quarter(peer)

        tiles(n_q, quarter)

    if chunks == 1:
        work(0)
    else:

        def work_step(at, carry):
            work(at)
            return carry

        lax.fori_loop(0, chunks, work_step, 0)
        loop(n_q, send_quarter)

    def scatter(matrix, values):
        return jnp.dot(matrix, values, preferred_element_type=F32)

    many(ownt_send, ownt_recv, n_q - 1, ownt_ss, ownt_rs).wait_recv()
    own_time = ownt_recv[...].reshape(n_q * item * 8, half)
    own_top = own_time.astype(BF)
    own_rest = (own_time - own_top.astype(F32)).astype(BF)
    own_sum = scatter(g_turn[1], own_top) + scatter(g_turn[1], own_rest)
    wait_block(
        lambda count: many(far_send, far_recv, count, far_ss, far_rs), lambda c: c.wait_recv()
    )
    summed = own_sum + scatter(g_turn[0], far_recv[...].reshape(n_b * rows, half))
    for h in range(2):
        at_row = h * 4 * sta
        out_ref[:, :, h * half : (h + 1) * half] = summed[at_row : at_row + 3 * sta].reshape(
            3, sta, half
        )

    many(g_send, g_recv, n_b - 1, g_ss, g_rs).wait_send()
    many(own_send, own_recv, n_q - 1, own_ss, own_rs).wait_send()
    many(ownt_send, ownt_recv, n_q - 1, ownt_ss, ownt_rs).wait_send()
    wait_block(
        lambda count: many(row_send, row_recv, count, row_ss, row_rs), lambda c: c.wait_send()
    )
    wait_block(
        lambda count: many(far_send, far_recv, count, far_ss, far_rs), lambda c: c.wait_send()
    )


def local(spectra, observed, own_station, partner_station, pair_count):
    n_b = lax.axis_size("blk")
    n_q = lax.axis_size("frq")
    sta = spectra.shape[2]
    band = spectra.shape[3]
    cap = own_station.shape[2]
    item = observed.shape[0]
    per = n_b // n_q
    rows = cap * 8
    cols = 8 * sta
    half = NT // n_q // 2
    chunk = min(item, 16)
    prow = -(-9 * chunk // 16) * 16
    scale = 1.0 / math.sqrt(2.0 * n_b * cap / sta)
    high, kept = tables()
    dma = pltpu.SemaphoreType.DMA
    held = pl.BlockSpec(memory_space=pltpu.HBM)
    out = pl.pallas_call(
        functools.partial(kernel, n_b, n_q, cap, sta, item, scale),
        out_shape=jax.ShapeDtypeStruct((3, sta, 2 * half), F32),
        in_specs=[held] * 7,
        out_specs=pl.BlockSpec(memory_space=pltpu.VMEM),
        scratch_shapes=[
            pltpu.SMEM((cap, n_b), jnp.int32),
            pltpu.SMEM((cap, n_b), jnp.int32),
            pltpu.SMEM((1, n_b), jnp.int32),
            pltpu.VMEM((2, 4, sta, band), BF),
            pltpu.VMEM((3, 3, item, NT), BF),
            pltpu.VMEM(high.shape, BF),
            pltpu.VMEM(kept.shape, BF),
            pltpu.VMEM((prow, 2 * LAG), F32),
            pltpu.VMEM((prow, 2 * LAG), F32),
            pltpu.VMEM((prow, 2 * NF), F32),
            pltpu.VMEM((n_b, rows, cols), BF),
            pltpu.VMEM((n_b, rows, cols), BF),
            pltpu.VMEM((n_b, rows, cols), BF),
            pltpu.VMEM((2, cols, n_b * rows), BF),
            pltpu.VMEM((n_q, item * 8, band), BF),
            pltpu.VMEM((n_q, item * 8, band), BF),
            pltpu.VMEM((n_b, rows, band), BF),
            pltpu.VMEM((n_q * per, rows, band), BF),
            pltpu.VMEM((n_q * per, rows, half), BF),
            pltpu.VMEM((n_b, rows, half), BF),
            pltpu.VMEM((n_q, item * 8, half), F32),
            pltpu.VMEM((n_q, item * 8, half), F32),
            dma((9,)),
            *[dma(())] * 10,
        ],
        compiler_params=pltpu.CompilerParams(
            collective_id=0, has_side_effects=True, vmem_limit_bytes=32 * 1024 * 1024
        ),
        cost_estimate=pl.CostEstimate(flops=400_000_000, bytes_accessed=6_000_000, transcendentals=0),
    )(
        *(
            pltpu.with_memory_space_constraint(operand, pltpu.HBM)
            for operand in (
                spectra,
                jnp.transpose(observed, (1, 2, 0, 3)),
                jnp.transpose(own_station[0], (1, 0)),
                jnp.transpose(partner_station[0], (1, 0)),
                pair_count,
                jnp.asarray(high),
                jnp.asarray(kept),
            )
        )
    )
    return jnp.transpose(out, (2, 0, 1))


def solution(mesh):
    return jax.shard_map(
        local,
        mesh=mesh,
        in_specs=(
            P(None, None, "blk", "frq"),
            P(("blk", "frq"), None, None, None),
            P("blk", None, None),
            P("blk", None, None),
            P("blk", None),
        ),
        out_specs=P("frq", None, "blk"),
        check_vma=False,
    )
```

```python
import functools
import math

import jax
import jax.numpy as jnp
import ml_dtypes
import numpy as np
from jax import lax
from jax.experimental import pallas as pl
from jax.experimental.pallas import tpu as pltpu
from jax.sharding import PartitionSpec as P

NF = 512
NT = 1024
LAG = NT // 4
MESH = pl.DeviceIdType.MESH
BF = jnp.bfloat16
F32 = jnp.float32


def tables():
    freq = np.arange(NF, dtype=np.int64)
    time = np.arange(NT, dtype=np.int64)
    num = (2 * freq + 1)[:, None] * time[None, :] % (2 * NT)
    phase = num.astype(np.float32) * np.float32(math.pi / NT)
    scale = np.float32(math.sqrt(NF))
    full = np.concatenate([np.cos(phase) / scale, -(np.sin(phase) / scale)], axis=0)
    high = full.astype(ml_dtypes.bfloat16)
    kept = np.concatenate([high[:, :LAG], high[:, NT - LAG :]], axis=1)
    return high, np.ascontiguousarray(kept.T)


def loop(count, body):
    if count <= 8:
        for step in range(count):
            body(step)
    else:

        def wrapped(step, carry):
            body(step)
            return carry

        lax.fori_loop(0, count, wrapped, 0)


def kernel(
    n_b, n_q, cap, sta, item, scale,
    spec_ref, obs_ref, own_in, part_in, cnt_in, high_ref, kept_ref,
    out_ref,
    own_ref, part_ref, cnt_ref, spec, obs, high, kept, obsf,
    g_send, g_recv, g_own, g_turn, own_send, own_recv, row_send, row_recv,
    far_send, far_recv, ownt_send, ownt_recv,
    local_sem, g_ss, g_rs, own_ss, own_rs, row_ss, row_rs, far_ss, far_rs, ownt_ss, ownt_rs,
):
    per = n_b // n_q
    rows = cap * 8
    cols = 8 * sta
    band = NF // n_q
    half = NT // n_q // 2
    chunk = min(item, 16)
    chunks = item // chunk
    prow = -(-9 * chunk // 16) * 16
    blocks = chunk // cap
    bits = chunk.bit_length() - 1
    b = lax.axis_index("blk")
    q = lax.axis_index("frq")
    home = lax.div(b, per)
    slot_in = lax.rem(b, per)

    def wrap(value, size):
        return jnp.where(value >= size, value - size, value)

    def other(here, step, size):
        if not isinstance(step, int):
            return wrap(here + 1 + step, size)
        order = sorted(range(1, size), key=lambda o: -min(o, size - o)) + [0]
        return wrap(here + order[step], size)

    id_loads = [
        pltpu.make_async_copy(part_in, part_ref, local_sem.at[5]),
        pltpu.make_async_copy(own_in, own_ref, local_sem.at[6]),
        pltpu.make_async_copy(cnt_in, cnt_ref, local_sem.at[7]),
    ]
    for load in id_loads:
        load.start()
    loads = [
        pltpu.make_async_copy(spec_ref.at[0], spec.at[0, pl.ds(0, 3)], local_sem.at[0]),
        pltpu.make_async_copy(spec_ref.at[1], spec.at[1, pl.ds(0, 3)], local_sem.at[1]),
        pltpu.make_async_copy(obs_ref, obs, local_sem.at[2]),
        pltpu.make_async_copy(
            high_ref.at[pl.ds(0, NF)], high.at[pl.ds(0, NF)], local_sem.at[3]
        ),
        pltpu.make_async_copy(
            high_ref.at[pl.ds(NF, NF)], high.at[pl.ds(NF, NF)], local_sem.at[4]
        ),
        pltpu.make_async_copy(kept_ref, kept, local_sem.at[8]),
    ]
    barrier = pltpu.get_barrier_semaphore()

    def greet(step):
        pl.semaphore_signal(
            barrier, inc=1, device_id=(other(b, step, n_b), q), device_id_type=MESH
        )

    for step in range(n_q - 1):
        pl.semaphore_signal(
            barrier, inc=1, device_id=(b, other(q, step, n_q)), device_id_type=MESH
        )
    loop(n_b - 1, greet)
    for load in loads:
        load.start()

    row_i = lax.broadcasted_iota(jnp.int32, (rows, cols), 0)
    col_i = lax.broadcasted_iota(jnp.int32, (rows, cols), 1)
    row_s = row_i >> 3
    base = col_i - (row_i & 7) * sta

    def pick(ids, block):
        chosen = jnp.full((rows, cols), ids[0, block], jnp.int32)
        for s in range(1, cap):
            chosen = jnp.where(row_s == s, ids[s, block], chosen)
        return jnp.where(base == chosen, 1.0, 0.0).astype(BF)

    def build(block):
        g_send[block] = pick(part_ref, block)

    def build_own(block):
        g_own[block] = pick(own_ref, block)

    for load in id_loads:
        load.wait()
    loop(n_b, build)
    pl.semaphore_wait(barrier, n_b + n_q - 2)

    def many(src, dst, count, send_sem, recv_sem):
        return pltpu.make_async_remote_copy(
            src_ref=src.at[pl.ds(0, count)], dst_ref=dst.at[pl.ds(0, count)], send_sem=send_sem,
            recv_sem=recv_sem, device_id=(wrap(b + 1, n_b), q), device_id_type=MESH,
        )

    def wait_block(copy_of, wait):
        @pl.when(q == home)
        def _():
            wait(copy_of(n_b - 1))

        @pl.when(q != home)
        def _():
            wait(copy_of(n_b))

    def g_copy(block, slot):
        return pltpu.make_async_remote_copy(
            src_ref=g_send.at[block], dst_ref=g_recv.at[slot], send_sem=g_ss,
            recv_sem=g_rs, device_id=(block, q), device_id_type=MESH,
        )

    def g_start(step):
        block = other(b, step, n_b)
        g_copy(block, b).start()

    loop(n_b - 1, g_start)
    g_recv[b] = g_send[b]

    loop(n_b, build_own)
    spec[0, 3] = jnp.zeros((sta, band), BF)
    spec[1, 3] = jnp.zeros((sta, band), BF)
    loads[0].wait()
    loads[1].wait()
    station_rows = spec[...].reshape(cols, band)

    def own_copy(peer, slot):
        return pltpu.make_async_remote_copy(
            src_ref=own_send.at[peer], dst_ref=own_recv.at[slot], send_sem=own_ss,
            recv_sem=own_rs, device_id=(b, peer), device_id_type=MESH,
        )

    picked = jnp.dot(
        g_own[...].reshape(n_b * rows, cols), station_rows, preferred_element_type=F32
    ).astype(BF)
    own_send[...] = picked.reshape(n_q, item * 8, band)
    for step in range(n_q - 1):
        own_copy(other(q, step, n_q), q).start()
    own_recv[q] = own_send[q]

    p_i = lax.broadcasted_iota(jnp.int32, (prow, 1), 0)
    p_ae = p_i >> bits
    p_slot = p_i & (chunk - 1)
    p_a = sum((p_ae >= 3 * m).astype(jnp.int32) for m in (1, 2, 3))
    p_e = jnp.where(p_ae >= 9, 3, p_ae - 3 * p_a)
    e_col = lax.broadcasted_iota(jnp.int32, (prow, chunk * 8), 1)

    def expand(component):
        want = p_slot * 8 + component
        return jnp.concatenate(
            [jnp.where(e_col == want + 4 * ri, 1.0, 0.0) for ri in range(2)], axis=0
        ).astype(BF)

    expand_u = expand(p_a)
    expand_v = expand(p_e)
    s_row = lax.broadcasted_iota(jnp.int32, (chunk * 8, prow), 0)
    s_col = lax.broadcasted_iota(jnp.int32, (chunk * 8, prow), 1)
    s_ae = s_col >> bits
    s_a = sum((s_ae >= 3 * m).astype(jnp.int32) for m in (1, 2, 3))
    s_e = jnp.where(s_ae >= 9, 3, s_ae - 3 * s_a)
    s_same = (s_row >> 3) == (s_col & (chunk - 1))
    s_comp = s_row & 3
    sum_e = jnp.where(s_same & (s_a == s_comp), 1.0, 0.0)
    sum_a = jnp.where(s_same & (s_e == s_comp), 1.0, 0.0)
    none = jnp.zeros((chunk * 8, prow), F32)
    sums = jnp.concatenate(
        [
            jnp.concatenate([sum_e, sum_e, none, none], axis=1),
            jnp.concatenate([none, none, sum_a, sum_a], axis=1),
        ],
        axis=0,
    ).astype(BF)
    lane = lax.broadcasted_iota(jnp.int32, (prow, 2 * LAG), 1)
    lag = jnp.where(lane < LAG, lane, 2 * LAG - lane)
    in_window = (lag >= NT // 32) & (lag < NT // 4)

    def prepare(at):
        if prow > 9 * chunk:
            obsf[9 * chunk :, :] = jnp.zeros((prow - 9 * chunk, 2 * LAG), F32)
        for a in range(3):
            for e in range(3):
                slab = obs[a, e, pl.ds(at * chunk, chunk), :] if chunks > 1 else obs[a, e]
                at_row = (3 * a + e) * chunk
                obsf[at_row : at_row + chunk, :LAG] = slab[:, :LAG].astype(F32)
                obsf[at_row : at_row + chunk, LAG:] = slab[:, NT - LAG :].astype(F32)

    loads[2].wait()
    if chunks == 1:
        prepare(0)

    many(g_send, g_recv, n_b - 1, g_ss, g_rs).wait_recv()
    row_send[...] = jnp.dot(
        g_recv[...].reshape(n_b * rows, cols), station_rows, preferred_element_type=F32
    ).astype(BF).reshape(n_b, rows, band)

    def row_copy(block, slot):
        return pltpu.make_async_remote_copy(
            src_ref=row_send.at[block], dst_ref=row_recv.at[slot], send_sem=row_ss,
            recv_sem=row_rs, device_id=(block, home), device_id_type=MESH,
        )

    mine = q * per + slot_in

    def row_start(step):
        row_copy(other(b, step, n_b), mine).start()

    loop(n_b - 1, row_start)

    @pl.when(q != home)
    def _():
        row_copy(b, mine).start()

    @pl.when(q == home)
    def _():
        row_recv[mine] = row_send[b]

    turn_i = lax.broadcasted_iota(jnp.int32, (cols, cols), 0)
    turn_j = lax.broadcasted_iota(jnp.int32, (cols, cols), 1)
    eye = jnp.where(turn_i == turn_j, 1.0, 0.0).astype(BF)

    def turned(matrix):
        return lax.dot_general(
            eye, matrix[...].reshape(n_b * rows, cols), (((1,), (1,)), ((), ())),
            preferred_element_type=F32,
        ).astype(BF)

    g_turn[0] = turned(g_recv)
    g_turn[1] = turned(g_own)
    many(own_send, own_recv, n_q - 1, own_ss, own_rs).wait_recv()

    def spread(matrix, parts):
        both = jnp.dot(matrix, jnp.concatenate(parts, axis=1), preferred_element_type=F32)
        return both[:prow], both[prow:]

    def spread_own(at):
        return spread(
            expand_u,
            [own_recv[p, pl.ds(at * chunk * 8, chunk * 8), :] for p in range(n_q)],
        )

    def first_part(at):
        alive = jnp.zeros((prow, 1), jnp.int32)
        for i in range(chunk):
            count = cnt_ref[0, q * per + at * blocks + i // cap]
            live = jnp.clip(count - i % cap, 0, 1)
            alive = jnp.where(p_slot == i, live, alive)
        alive = jnp.where(p_ae < 9, alive, 0)
        alive_f = alive.astype(F32)
        keep = in_window & (alive > 0)
        ur, ui = spread_own(at)
        return ur, ui, alive_f, keep

    early = first_part(0) if chunks == 1 else None
    wait_block(
        lambda count: many(row_send, row_recv, count, row_ss, row_rs), lambda c: c.wait_recv()
    )
    for load in loads[3:]:
        load.wait()

    def far_copy(peer, inner, slot):
        return pltpu.make_async_remote_copy(
            src_ref=far_send.at[peer * per + inner], dst_ref=far_recv.at[slot],
            send_sem=far_ss, recv_sem=far_rs,
            device_id=(q * per + inner, peer), device_id_type=MESH,
        )

    def ownt_copy(peer, slot):
        return pltpu.make_async_remote_copy(
            src_ref=ownt_send.at[peer], dst_ref=ownt_recv.at[slot], send_sem=ownt_ss,
            recv_sem=ownt_rs, device_id=(b, peer), device_id_type=MESH,
        )

    def send_quarter(peer):
        def far_start(inner):
            away = jnp.logical_or(q * per + inner != b, q != peer)

            @pl.when(away)
            def _():
                far_copy(peer, inner, b).start()

            @pl.when(jnp.logical_not(away))
            def _():
                far_recv[b] = far_send[peer * per + inner]

        loop(per, far_start)

        @pl.when(q != peer)
        def _():
            ownt_copy(peer, q).start()

        @pl.when(q == peer)
        def _():
            ownt_recv[peer] = ownt_send[peer]

    def work(at):
        if chunks > 1:
            prepare(at)
        ur, ui, alive_f, keep = early if chunks == 1 else first_part(at)
        vr, vi = spread(
            expand_v,
            [
                row_recv[pl.ds(p * per + at * blocks, blocks)].reshape(chunk * 8, band)
                for p in range(n_q)
            ],
        )
        cross = jnp.concatenate(
            [(ur * vr + ui * vi) * alive_f, (ui * vr - ur * vi) * alive_f], axis=1
        ).astype(BF)
        correlation = jnp.concatenate(
            [
                jnp.dot(cross, high[:, :LAG], preferred_element_type=F32),
                jnp.dot(cross, high[:, NT - LAG :], preferred_element_type=F32),
            ],
            axis=1,
        )
        residual = jnp.where(keep, correlation - obsf[...], 0.0).astype(BF)
        adj = jnp.dot(residual, kept[...], preferred_element_type=F32).astype(BF).astype(F32)
        ar, ai = adj[:, :NF], adj[:, NF:]

        def halves(real, imag):
            terms = jnp.concatenate([real, imag], axis=1)
            upper = terms.astype(BF)
            return [upper, (terms - upper.astype(F32)).astype(BF)]

        terms = jnp.concatenate(
            halves(ar * vr - ai * vi, ar * vi + ai * vr)
            + halves(ar * ur + ai * ui, ar * ui - ai * ur),
            axis=0,
        )
        grad = jnp.dot(sums, terms, preferred_element_type=F32)
        top = grad.astype(BF)
        rest = (grad - top.astype(F32)).astype(BF)
        stacked = jnp.concatenate([top, rest], axis=0)
        count = chunk * 16
        first_half = (lax.broadcasted_iota(jnp.int32, (count, half), 0) & 7) < 4
        for step in range(n_q):
            peer = other(q, step, n_q)
            column = pl.ds(pl.multiple_of(peer * 2 * half, 2 * half), 2 * half)
            product = jnp.dot(stacked, high[:, column], preferred_element_type=F32)
            product = (product[:count] + product[count:]) * scale
            message = jnp.where(first_half, product[:, :half], product[:, half:])
            ownt_send[peer, pl.ds(at * chunk * 8, chunk * 8), :] = message[: chunk * 8].astype(BF)
            far_send[pl.ds(peer * per + at * blocks, blocks)] = (
                message[chunk * 8 :].astype(BF).reshape(blocks, rows, half)
            )
            if chunks == 1:
                send_quarter(peer)

    if chunks == 1:
        work(0)
    else:

        def work_step(at, carry):
            work(at)
            return carry

        lax.fori_loop(0, chunks, work_step, 0)
        for peer in range(n_q):
            send_quarter(peer)

    def scatter(matrix, values):
        return jnp.dot(matrix, values, preferred_element_type=F32)

    many(ownt_send, ownt_recv, n_q - 1, ownt_ss, ownt_rs).wait_recv()
    own_sum = scatter(g_turn[1], ownt_recv[...].reshape(n_q * item * 8, half))
    wait_block(
        lambda count: many(far_send, far_recv, count, far_ss, far_rs), lambda c: c.wait_recv()
    )
    summed = own_sum + scatter(g_turn[0], far_recv[...].reshape(n_b * rows, half))
    for h in range(2):
        at_row = h * 4 * sta
        out_ref[:, :, h * half : (h + 1) * half] = summed[at_row : at_row + 3 * sta].reshape(
            3, sta, half
        )

    many(g_send, g_recv, n_b - 1, g_ss, g_rs).wait_send()
    many(own_send, own_recv, n_q - 1, own_ss, own_rs).wait_send()
    many(ownt_send, ownt_recv, n_q - 1, ownt_ss, ownt_rs).wait_send()
    wait_block(
        lambda count: many(row_send, row_recv, count, row_ss, row_rs), lambda c: c.wait_send()
    )
    wait_block(
        lambda count: many(far_send, far_recv, count, far_ss, far_rs), lambda c: c.wait_send()
    )


def local(spectra, observed, own_station, partner_station, pair_count):
    n_b = lax.axis_size("blk")
    n_q = lax.axis_size("frq")
    sta = spectra.shape[2]
    band = spectra.shape[3]
    cap = own_station.shape[2]
    item = observed.shape[0]
    per = n_b // n_q
    rows = cap * 8
    cols = 8 * sta
    half = NT // n_q // 2
    chunk = min(item, 16)
    prow = -(-9 * chunk // 16) * 16
    scale = 1.0 / math.sqrt(2.0 * n_b * cap / sta)
    high, kept = tables()
    dma = pltpu.SemaphoreType.DMA
    held = pl.BlockSpec(memory_space=pltpu.HBM)
    out = pl.pallas_call(
        functools.partial(kernel, n_b, n_q, cap, sta, item, scale),
        out_shape=jax.ShapeDtypeStruct((3, sta, 2 * half), F32),
        in_specs=[held] * 7,
        out_specs=pl.BlockSpec(memory_space=pltpu.VMEM),
        scratch_shapes=[
            pltpu.SMEM((cap, n_b), jnp.int32),
            pltpu.SMEM((cap, n_b), jnp.int32),
            pltpu.SMEM((1, n_b), jnp.int32),
            pltpu.VMEM((2, 4, sta, band), BF),
            pltpu.VMEM((3, 3, item, NT), BF),
            pltpu.VMEM(high.shape, BF),
            pltpu.VMEM(kept.shape, BF),
            pltpu.VMEM((prow, 2 * LAG), F32),
            pltpu.VMEM((n_b, rows, cols), BF),
            pltpu.VMEM((n_b, rows, cols), BF),
            pltpu.VMEM((n_b, rows, cols), BF),
            pltpu.VMEM((2, cols, n_b * rows), BF),
            pltpu.VMEM((n_q, item * 8, band), BF),
            pltpu.VMEM((n_q, item * 8, band), BF),
            pltpu.VMEM((n_b, rows, band), BF),
            pltpu.VMEM((n_q * per, rows, band), BF),
            pltpu.VMEM((n_q * per, rows, half), BF),
            pltpu.VMEM((n_b, rows, half), BF),
            pltpu.VMEM((n_q, item * 8, half), BF),
            pltpu.VMEM((n_q, item * 8, half), BF),
            dma((9,)),
            *[dma(())] * 10,
        ],
        compiler_params=pltpu.CompilerParams(
            collective_id=0, has_side_effects=True, vmem_limit_bytes=32 * 1024 * 1024
        ),
        cost_estimate=pl.CostEstimate(flops=400_000_000, bytes_accessed=6_000_000, transcendentals=0),
    )(
        *(
            pltpu.with_memory_space_constraint(operand, pltpu.HBM)
            for operand in (
                spectra,
                jnp.transpose(observed, (1, 2, 0, 3)),
                jnp.transpose(own_station[0], (1, 0)),
                jnp.transpose(partner_station[0], (1, 0)),
                pair_count,
                jnp.asarray(high),
                jnp.asarray(kept),
            )
        )
    )
    return jnp.transpose(out, (2, 0, 1))


def solution(mesh):
    return jax.shard_map(
        local,
        mesh=mesh,
        in_specs=(
            P(None, None, "blk", "frq"),
            P(("blk", "frq"), None, None, None),
            P("blk", None, None),
            P("blk", None, None),
            P("blk", None),
        ),
        out_specs=P("frq", None, "blk"),
        check_vma=False,
    )
```

```python
import functools
import math

import jax
import jax.numpy as jnp
import ml_dtypes
import numpy as np
from jax import lax
from jax.experimental import pallas as pl
from jax.experimental.pallas import tpu as pltpu
from jax.sharding import PartitionSpec as P

NF = 512
NT = 1024
LAG = NT // 4
MESH = pl.DeviceIdType.MESH
BF = jnp.bfloat16
F32 = jnp.float32


def tables():
    freq = np.arange(NF, dtype=np.int64)
    time = np.arange(NT, dtype=np.int64)
    num = (2 * freq + 1)[:, None] * time[None, :] % (2 * NT)
    phase = num.astype(np.float32) * np.float32(math.pi / NT)
    scale = np.float32(math.sqrt(NF))
    full = np.concatenate([np.cos(phase) / scale, -(np.sin(phase) / scale)], axis=0)
    high = full.astype(ml_dtypes.bfloat16)
    kept = np.concatenate([high[:, :LAG], high[:, NT - LAG :]], axis=1)
    return high, np.ascontiguousarray(kept.T)


def loop(count, body):
    if count <= 8:
        for step in range(count):
            body(step)
    else:

        def wrapped(step, carry):
            body(step)
            return carry

        lax.fori_loop(0, count, wrapped, 0)


def kernel(
    n_b, n_q, cap, sta, item, scale,
    spec_ref, obs_ref, own_in, part_in, cnt_in, high_ref, kept_ref,
    out_ref,
    own_ref, part_ref, cnt_ref, spec, obs, high, kept, obsf,
    g_send, g_recv, g_own, g_turn, own_send, own_recv, row_send, row_recv,
    far_send, far_recv, ownt_send, ownt_recv,
    local_sem, g_ss, g_rs, own_ss, own_rs, row_ss, row_rs, far_ss, far_rs, ownt_ss, ownt_rs,
):
    per = n_b // n_q
    rows = cap * 8
    cols = 8 * sta
    band = NF // n_q
    half = NT // n_q // 2
    chunk = min(item, 16)
    chunks = item // chunk
    prow = -(-9 * chunk // 16) * 16
    blocks = chunk // cap
    bits = chunk.bit_length() - 1
    b = lax.axis_index("blk")
    q = lax.axis_index("frq")
    home = lax.div(b, per)
    slot_in = lax.rem(b, per)

    def wrap(value, size):
        return jnp.where(value >= size, value - size, value)

    id_loads = [
        pltpu.make_async_copy(part_in, part_ref, local_sem.at[5]),
        pltpu.make_async_copy(own_in, own_ref, local_sem.at[6]),
        pltpu.make_async_copy(cnt_in, cnt_ref, local_sem.at[7]),
    ]
    for load in id_loads:
        load.start()
    loads = [
        pltpu.make_async_copy(spec_ref.at[0], spec.at[0, pl.ds(0, 3)], local_sem.at[0]),
        pltpu.make_async_copy(spec_ref.at[1], spec.at[1, pl.ds(0, 3)], local_sem.at[1]),
        pltpu.make_async_copy(obs_ref, obs, local_sem.at[2]),
        pltpu.make_async_copy(
            high_ref.at[pl.ds(0, NF)], high.at[pl.ds(0, NF)], local_sem.at[3]
        ),
        pltpu.make_async_copy(
            high_ref.at[pl.ds(NF, NF)], high.at[pl.ds(NF, NF)], local_sem.at[4]
        ),
        pltpu.make_async_copy(kept_ref, kept, local_sem.at[8]),
    ]
    barrier = pltpu.get_barrier_semaphore()

    def greet(step):
        pl.semaphore_signal(
            barrier, inc=1, device_id=(wrap(b + 1 + step, n_b), q), device_id_type=MESH
        )

    for step in range(n_q - 1):
        pl.semaphore_signal(
            barrier, inc=1, device_id=(b, wrap(q + 1 + step, n_q)), device_id_type=MESH
        )
    loop(n_b - 1, greet)
    for load in loads:
        load.start()

    row_i = lax.broadcasted_iota(jnp.int32, (rows, cols), 0)
    col_i = lax.broadcasted_iota(jnp.int32, (rows, cols), 1)
    row_s = row_i >> 3
    base = col_i - (row_i & 7) * sta

    def pick(ids, block):
        chosen = jnp.full((rows, cols), ids[0, block], jnp.int32)
        for s in range(1, cap):
            chosen = jnp.where(row_s == s, ids[s, block], chosen)
        return jnp.where(base == chosen, 1.0, 0.0).astype(BF)

    def build(block):
        g_send[block] = pick(part_ref, block)

    def build_own(block):
        g_own[block] = pick(own_ref, block)

    for load in id_loads:
        load.wait()
    loop(n_b, build)
    pl.semaphore_wait(barrier, n_b + n_q - 2)

    def many(src, dst, count, send_sem, recv_sem):
        return pltpu.make_async_remote_copy(
            src_ref=src.at[pl.ds(0, count)], dst_ref=dst.at[pl.ds(0, count)], send_sem=send_sem,
            recv_sem=recv_sem, device_id=(wrap(b + 1, n_b), q), device_id_type=MESH,
        )

    def wait_block(copy_of, wait):
        @pl.when(q == home)
        def _():
            wait(copy_of(n_b - 1))

        @pl.when(q != home)
        def _():
            wait(copy_of(n_b))

    def g_copy(block, slot):
        return pltpu.make_async_remote_copy(
            src_ref=g_send.at[block], dst_ref=g_recv.at[slot], send_sem=g_ss,
            recv_sem=g_rs, device_id=(block, q), device_id_type=MESH,
        )

    def g_start(step):
        block = wrap(b + 1 + step, n_b)
        g_copy(block, b).start()

    loop(n_b - 1, g_start)
    g_recv[b] = g_send[b]

    loop(n_b, build_own)
    spec[0, 3] = jnp.zeros((sta, band), BF)
    spec[1, 3] = jnp.zeros((sta, band), BF)
    loads[0].wait()
    loads[1].wait()
    station_rows = spec[...].reshape(cols, band)

    def own_copy(peer, slot):
        return pltpu.make_async_remote_copy(
            src_ref=own_send.at[peer], dst_ref=own_recv.at[slot], send_sem=own_ss,
            recv_sem=own_rs, device_id=(b, peer), device_id_type=MESH,
        )

    picked = jnp.dot(
        g_own[...].reshape(n_b * rows, cols), station_rows, preferred_element_type=F32
    ).astype(BF)
    own_send[...] = picked.reshape(n_q, item * 8, band)
    for step in range(n_q - 1):
        own_copy(wrap(q + 1 + step, n_q), q).start()
    own_recv[q] = own_send[q]

    p_i = lax.broadcasted_iota(jnp.int32, (prow, 1), 0)
    p_ae = p_i >> bits
    p_slot = p_i & (chunk - 1)
    p_a = sum((p_ae >= 3 * m).astype(jnp.int32) for m in (1, 2, 3))
    p_e = jnp.where(p_ae >= 9, 3, p_ae - 3 * p_a)
    e_col = lax.broadcasted_iota(jnp.int32, (prow, chunk * 8), 1)

    def expand(component):
        want = p_slot * 8 + component
        return jnp.concatenate(
            [jnp.where(e_col == want + 4 * ri, 1.0, 0.0) for ri in range(2)], axis=0
        ).astype(BF)

    expand_u = expand(p_a)
    expand_v = expand(p_e)
    s_row = lax.broadcasted_iota(jnp.int32, (chunk * 8, prow), 0)
    s_col = lax.broadcasted_iota(jnp.int32, (chunk * 8, prow), 1)
    s_ae = s_col >> bits
    s_a = sum((s_ae >= 3 * m).astype(jnp.int32) for m in (1, 2, 3))
    s_e = jnp.where(s_ae >= 9, 3, s_ae - 3 * s_a)
    s_same = (s_row >> 3) == (s_col & (chunk - 1))
    s_comp = s_row & 3
    sum_e = jnp.where(s_same & (s_a == s_comp), 1.0, 0.0)
    sum_a = jnp.where(s_same & (s_e == s_comp), 1.0, 0.0)
    none = jnp.zeros((chunk * 8, prow), F32)
    sums = jnp.concatenate(
        [
            jnp.concatenate([sum_e, sum_e, none, none], axis=1),
            jnp.concatenate([none, none, sum_a, sum_a], axis=1),
        ],
        axis=0,
    ).astype(BF)
    lane = lax.broadcasted_iota(jnp.int32, (prow, 2 * LAG), 1)
    lag = jnp.where(lane < LAG, lane, 2 * LAG - lane)
    in_window = (lag >= NT // 32) & (lag < NT // 4)

    def prepare(at):
        if prow > 9 * chunk:
            obsf[9 * chunk :, :] = jnp.zeros((prow - 9 * chunk, 2 * LAG), F32)
        for a in range(3):
            for e in range(3):
                slab = obs[a, e, pl.ds(at * chunk, chunk), :] if chunks > 1 else obs[a, e]
                at_row = (3 * a + e) * chunk
                obsf[at_row : at_row + chunk, :LAG] = slab[:, :LAG].astype(F32)
                obsf[at_row : at_row + chunk, LAG:] = slab[:, NT - LAG :].astype(F32)

    loads[2].wait()
    if chunks == 1:
        prepare(0)

    many(g_send, g_recv, n_b - 1, g_ss, g_rs).wait_recv()
    row_send[...] = jnp.dot(
        g_recv[...].reshape(n_b * rows, cols), station_rows, preferred_element_type=F32
    ).astype(BF).reshape(n_b, rows, band)

    def row_copy(block, slot):
        return pltpu.make_async_remote_copy(
            src_ref=row_send.at[block], dst_ref=row_recv.at[slot], send_sem=row_ss,
            recv_sem=row_rs, device_id=(block, home), device_id_type=MESH,
        )

    mine = q * per + slot_in

    def row_start(step):
        row_copy(wrap(b + 1 + step, n_b), mine).start()

    loop(n_b - 1, row_start)

    @pl.when(q != home)
    def _():
        row_copy(b, mine).start()

    @pl.when(q == home)
    def _():
        row_recv[mine] = row_send[b]

    turn_i = lax.broadcasted_iota(jnp.int32, (cols, cols), 0)
    turn_j = lax.broadcasted_iota(jnp.int32, (cols, cols), 1)
    eye = jnp.where(turn_i == turn_j, 1.0, 0.0).astype(BF)

    def turned(matrix):
        return lax.dot_general(
            eye, matrix[...].reshape(n_b * rows, cols), (((1,), (1,)), ((), ())),
            preferred_element_type=F32,
        ).astype(BF)

    g_turn[0] = turned(g_recv)
    g_turn[1] = turned(g_own)
    many(own_send, own_recv, n_q - 1, own_ss, own_rs).wait_recv()

    def spread(matrix, parts):
        both = jnp.dot(matrix, jnp.concatenate(parts, axis=1), preferred_element_type=F32)
        return both[:prow], both[prow:]

    def spread_own(at):
        return spread(
            expand_u,
            [own_recv[p, pl.ds(at * chunk * 8, chunk * 8), :] for p in range(n_q)],
        )

    def first_part(at):
        alive = jnp.zeros((prow, 1), jnp.int32)
        for i in range(chunk):
            count = cnt_ref[0, q * per + at * blocks + i // cap]
            live = jnp.clip(count - i % cap, 0, 1)
            alive = jnp.where(p_slot == i, live, alive)
        alive = jnp.where(p_ae < 9, alive, 0)
        alive_f = alive.astype(F32)
        keep = in_window & (alive > 0)
        ur, ui = spread_own(at)
        return ur, ui, alive_f, keep

    early = first_part(0) if chunks == 1 else None
    wait_block(
        lambda count: many(row_send, row_recv, count, row_ss, row_rs), lambda c: c.wait_recv()
    )
    for load in loads[3:]:
        load.wait()

    def far_copy(peer, inner, slot):
        return pltpu.make_async_remote_copy(
            src_ref=far_send.at[peer * per + inner], dst_ref=far_recv.at[slot],
            send_sem=far_ss, recv_sem=far_rs,
            device_id=(q * per + inner, peer), device_id_type=MESH,
        )

    def ownt_copy(peer, slot):
        return pltpu.make_async_remote_copy(
            src_ref=ownt_send.at[peer], dst_ref=ownt_recv.at[slot], send_sem=ownt_ss,
            recv_sem=ownt_rs, device_id=(b, peer), device_id_type=MESH,
        )

    def send_quarter(peer):
        def far_start(inner):
            other = jnp.logical_or(q * per + inner != b, q != peer)

            @pl.when(other)
            def _():
                far_copy(peer, inner, b).start()

            @pl.when(jnp.logical_not(other))
            def _():
                far_recv[b] = far_send[peer * per + inner]

        loop(per, far_start)

        @pl.when(q != peer)
        def _():
            ownt_copy(peer, q).start()

        @pl.when(q == peer)
        def _():
            ownt_recv[peer] = ownt_send[peer]

    def work(at):
        if chunks > 1:
            prepare(at)
        ur, ui, alive_f, keep = early if chunks == 1 else first_part(at)
        vr, vi = spread(
            expand_v,
            [
                row_recv[pl.ds(p * per + at * blocks, blocks)].reshape(chunk * 8, band)
                for p in range(n_q)
            ],
        )
        cross = jnp.concatenate(
            [(ur * vr + ui * vi) * alive_f, (ui * vr - ur * vi) * alive_f], axis=1
        ).astype(BF)
        correlation = jnp.concatenate(
            [
                jnp.dot(cross, high[:, :LAG], preferred_element_type=F32),
                jnp.dot(cross, high[:, NT - LAG :], preferred_element_type=F32),
            ],
            axis=1,
        )
        residual = jnp.where(keep, correlation - obsf[...], 0.0).astype(BF)
        adj = jnp.dot(residual, kept[...], preferred_element_type=F32).astype(BF).astype(F32)
        ar, ai = adj[:, :NF], adj[:, NF:]

        def halves(real, imag):
            terms = jnp.concatenate([real, imag], axis=1)
            upper = terms.astype(BF)
            return [upper, (terms - upper.astype(F32)).astype(BF)]

        terms = jnp.concatenate(
            halves(ar * vr - ai * vi, ar * vi + ai * vr)
            + halves(ar * ur + ai * ui, ar * ui - ai * ur),
            axis=0,
        )
        grad = jnp.dot(sums, terms, preferred_element_type=F32)
        top = grad.astype(BF)
        rest = (grad - top.astype(F32)).astype(BF)
        stacked = jnp.concatenate([top, rest], axis=0)
        count = chunk * 16
        first_half = (lax.broadcasted_iota(jnp.int32, (count, half), 0) & 7) < 4
        product = jnp.dot(stacked, high[...], preferred_element_type=F32)
        product = (product[:count] + product[count:]) * scale
        for peer in range(n_q):
            at_col = peer * 2 * half
            message = jnp.where(
                first_half,
                product[:, at_col : at_col + half],
                product[:, at_col + half : at_col + 2 * half],
            )
            ownt_send[peer, pl.ds(at * chunk * 8, chunk * 8), :] = message[: chunk * 8]
            far_send[pl.ds(peer * per + at * blocks, blocks)] = (
                message[chunk * 8 :].astype(BF).reshape(blocks, rows, half)
            )
        if chunks == 1:
            for peer in range(n_q):
                send_quarter(peer)

    if chunks == 1:
        work(0)
    else:

        def work_step(at, carry):
            work(at)
            return carry

        lax.fori_loop(0, chunks, work_step, 0)
        for peer in range(n_q):
            send_quarter(peer)

    def scatter(matrix, values):
        return jnp.dot(matrix, values, preferred_element_type=F32)

    many(ownt_send, ownt_recv, n_q - 1, ownt_ss, ownt_rs).wait_recv()
    own_time = ownt_recv[...].reshape(n_q * item * 8, half)
    own_top = own_time.astype(BF)
    own_rest = (own_time - own_top.astype(F32)).astype(BF)
    own_sum = scatter(g_turn[1], own_top) + scatter(g_turn[1], own_rest)
    wait_block(
        lambda count: many(far_send, far_recv, count, far_ss, far_rs), lambda c: c.wait_recv()
    )
    summed = own_sum + scatter(g_turn[0], far_recv[...].reshape(n_b * rows, half))
    for h in range(2):
        at_row = h * 4 * sta
        out_ref[:, :, h * half : (h + 1) * half] = summed[at_row : at_row + 3 * sta].reshape(
            3, sta, half
        )

    many(g_send, g_recv, n_b - 1, g_ss, g_rs).wait_send()
    many(own_send, own_recv, n_q - 1, own_ss, own_rs).wait_send()
    many(ownt_send, ownt_recv, n_q - 1, ownt_ss, ownt_rs).wait_send()
    wait_block(
        lambda count: many(row_send, row_recv, count, row_ss, row_rs), lambda c: c.wait_send()
    )
    wait_block(
        lambda count: many(far_send, far_recv, count, far_ss, far_rs), lambda c: c.wait_send()
    )


def local(spectra, observed, own_station, partner_station, pair_count):
    n_b = lax.axis_size("blk")
    n_q = lax.axis_size("frq")
    sta = spectra.shape[2]
    band = spectra.shape[3]
    cap = own_station.shape[2]
    item = observed.shape[0]
    per = n_b // n_q
    rows = cap * 8
    cols = 8 * sta
    half = NT // n_q // 2
    chunk = min(item, 16)
    prow = -(-9 * chunk // 16) * 16
    scale = 1.0 / math.sqrt(2.0 * n_b * cap / sta)
    high, kept = tables()
    dma = pltpu.SemaphoreType.DMA
    held = pl.BlockSpec(memory_space=pltpu.HBM)
    out = pl.pallas_call(
        functools.partial(kernel, n_b, n_q, cap, sta, item, scale),
        out_shape=jax.ShapeDtypeStruct((3, sta, 2 * half), F32),
        in_specs=[held] * 7,
        out_specs=pl.BlockSpec(memory_space=pltpu.VMEM),
        scratch_shapes=[
            pltpu.SMEM((cap, n_b), jnp.int32),
            pltpu.SMEM((cap, n_b), jnp.int32),
            pltpu.SMEM((1, n_b), jnp.int32),
            pltpu.VMEM((2, 4, sta, band), BF),
            pltpu.VMEM((3, 3, item, NT), BF),
            pltpu.VMEM(high.shape, BF),
            pltpu.VMEM(kept.shape, BF),
            pltpu.VMEM((prow, 2 * LAG), F32),
            pltpu.VMEM((n_b, rows, cols), BF),
            pltpu.VMEM((n_b, rows, cols), BF),
            pltpu.VMEM((n_b, rows, cols), BF),
            pltpu.VMEM((2, cols, n_b * rows), BF),
            pltpu.VMEM((n_q, item * 8, band), BF),
            pltpu.VMEM((n_q, item * 8, band), BF),
            pltpu.VMEM((n_b, rows, band), BF),
            pltpu.VMEM((n_q * per, rows, band), BF),
            pltpu.VMEM((n_q * per, rows, half), BF),
            pltpu.VMEM((n_b, rows, half), BF),
            pltpu.VMEM((n_q, item * 8, half), F32),
            pltpu.VMEM((n_q, item * 8, half), F32),
            dma((9,)),
            *[dma(())] * 10,
        ],
        compiler_params=pltpu.CompilerParams(
            collective_id=0, has_side_effects=True, vmem_limit_bytes=32 * 1024 * 1024
        ),
        cost_estimate=pl.CostEstimate(flops=400_000_000, bytes_accessed=6_000_000, transcendentals=0),
    )(
        *(
            pltpu.with_memory_space_constraint(operand, pltpu.HBM)
            for operand in (
                spectra,
                jnp.transpose(observed, (1, 2, 0, 3)),
                jnp.transpose(own_station[0], (1, 0)),
                jnp.transpose(partner_station[0], (1, 0)),
                pair_count,
                jnp.asarray(high),
                jnp.asarray(kept),
            )
        )
    )
    return jnp.transpose(out, (2, 0, 1))


def solution(mesh):
    return jax.shard_map(
        local,
        mesh=mesh,
        in_specs=(
            P(None, None, "blk", "frq"),
            P(("blk", "frq"), None, None, None),
            P("blk", None, None),
            P("blk", None, None),
            P("blk", None),
        ),
        out_specs=P("frq", None, "blk"),
        check_vma=False,
    )
```

```python
import functools
import math

import jax
import jax.numpy as jnp
import ml_dtypes
import numpy as np
from jax import lax
from jax.experimental import pallas as pl
from jax.experimental.pallas import tpu as pltpu
from jax.sharding import PartitionSpec as P

NF = 512
NT = 1024
LAG = NT // 4
MESH = pl.DeviceIdType.MESH
BF = jnp.bfloat16
F32 = jnp.float32


def tables():
    freq = np.arange(NF, dtype=np.int64)
    time = np.arange(NT, dtype=np.int64)
    num = (2 * freq + 1)[:, None] * time[None, :] % (2 * NT)
    phase = num.astype(np.float32) * np.float32(math.pi / NT)
    scale = np.float32(math.sqrt(NF))
    full = np.concatenate([np.cos(phase) / scale, -(np.sin(phase) / scale)], axis=0)
    high = full.astype(ml_dtypes.bfloat16)
    kept = np.concatenate([high[:, :LAG], high[:, NT - LAG :]], axis=1)
    return high, np.ascontiguousarray(kept.T)


def loop(count, body):
    if count <= 8:
        for step in range(count):
            body(step)
    else:

        def wrapped(step, carry):
            body(step)
            return carry

        lax.fori_loop(0, count, wrapped, 0)


def kernel(
    n_b, n_q, cap, sta, item, scale,
    spec_ref, obs_ref, own_in, part_in, cnt_in, high_ref, kept_ref,
    out_ref,
    own_ref, part_ref, cnt_ref, spec, obs, high, kept, obsf,
    g_send, g_recv, g_own, g_turn, own_send, own_recv, row_send, row_recv,
    far_send, far_recv, ownt_send, ownt_recv,
    local_sem, g_ss, g_rs, own_ss, own_rs, row_ss, row_rs, far_ss, far_rs, ownt_ss, ownt_rs,
):
    per = n_b // n_q
    rows = cap * 8
    cols = 8 * sta
    band = NF // n_q
    half = NT // n_q // 2
    chunk = min(item, 16)
    chunks = item // chunk
    prow = -(-9 * chunk // 16) * 16
    blocks = chunk // cap
    bits = chunk.bit_length() - 1
    b = lax.axis_index("blk")
    q = lax.axis_index("frq")
    home = lax.div(b, per)
    slot_in = lax.rem(b, per)

    def wrap(value, size):
        return jnp.where(value >= size, value - size, value)

    id_loads = [
        pltpu.make_async_copy(part_in, part_ref, local_sem.at[5]),
        pltpu.make_async_copy(own_in, own_ref, local_sem.at[6]),
        pltpu.make_async_copy(cnt_in, cnt_ref, local_sem.at[7]),
    ]
    for load in id_loads:
        load.start()
    loads = [
        pltpu.make_async_copy(spec_ref.at[0], spec.at[0, pl.ds(0, 3)], local_sem.at[0]),
        pltpu.make_async_copy(spec_ref.at[1], spec.at[1, pl.ds(0, 3)], local_sem.at[1]),
        pltpu.make_async_copy(obs_ref, obs, local_sem.at[2]),
        pltpu.make_async_copy(
            high_ref.at[pl.ds(0, NF)], high.at[pl.ds(0, NF)], local_sem.at[3]
        ),
        pltpu.make_async_copy(
            high_ref.at[pl.ds(NF, NF)], high.at[pl.ds(NF, NF)], local_sem.at[4]
        ),
        pltpu.make_async_copy(kept_ref, kept, local_sem.at[8]),
    ]
    barrier = pltpu.get_barrier_semaphore()

    def greet(step):
        pl.semaphore_signal(
            barrier, inc=1, device_id=(wrap(b + 1 + step, n_b), q), device_id_type=MESH
        )

    for step in range(n_q - 1):
        pl.semaphore_signal(
            barrier, inc=1, device_id=(b, wrap(q + 1 + step, n_q)), device_id_type=MESH
        )
    loop(n_b - 1, greet)
    for load in loads:
        load.start()

    row_i = lax.broadcasted_iota(jnp.int32, (rows, cols), 0)
    col_i = lax.broadcasted_iota(jnp.int32, (rows, cols), 1)
    row_s = row_i >> 3
    base = col_i - (row_i & 7) * sta

    def pick(ids, block):
        chosen = jnp.full((rows, cols), ids[0, block], jnp.int32)
        for s in range(1, cap):
            chosen = jnp.where(row_s == s, ids[s, block], chosen)
        return jnp.where(base == chosen, 1.0, 0.0).astype(BF)

    def build(block):
        g_send[block] = pick(part_ref, block)

    def build_own(block):
        g_own[block] = pick(own_ref, block)

    for load in id_loads:
        load.wait()
    loop(n_b, build)
    pl.semaphore_wait(barrier, n_b + n_q - 2)

    def many(src, dst, count, send_sem, recv_sem):
        return pltpu.make_async_remote_copy(
            src_ref=src.at[pl.ds(0, count)], dst_ref=dst.at[pl.ds(0, count)], send_sem=send_sem,
            recv_sem=recv_sem, device_id=(wrap(b + 1, n_b), q), device_id_type=MESH,
        )

    def wait_block(copy_of, wait):
        @pl.when(q == home)
        def _():
            wait(copy_of(n_b - 1))

        @pl.when(q != home)
        def _():
            wait(copy_of(n_b))

    def g_copy(block, slot):
        return pltpu.make_async_remote_copy(
            src_ref=g_send.at[block], dst_ref=g_recv.at[slot], send_sem=g_ss,
            recv_sem=g_rs, device_id=(block, q), device_id_type=MESH,
        )

    def g_start(step):
        block = wrap(b + 1 + step, n_b)
        g_copy(block, b).start()

    loop(n_b - 1, g_start)
    g_recv[b] = g_send[b]

    loop(n_b, build_own)
    spec[0, 3] = jnp.zeros((sta, band), BF)
    spec[1, 3] = jnp.zeros((sta, band), BF)
    loads[0].wait()
    loads[1].wait()
    station_rows = spec[...].reshape(cols, band)

    def own_copy(peer, slot):
        return pltpu.make_async_remote_copy(
            src_ref=own_send.at[peer], dst_ref=own_recv.at[slot], send_sem=own_ss,
            recv_sem=own_rs, device_id=(b, peer), device_id_type=MESH,
        )

    picked = jnp.dot(
        g_own[...].reshape(n_b * rows, cols), station_rows, preferred_element_type=F32
    ).astype(BF)
    own_send[...] = picked.reshape(n_q, item * 8, band)
    for step in range(n_q - 1):
        own_copy(wrap(q + 1 + step, n_q), q).start()
    own_recv[q] = own_send[q]

    p_i = lax.broadcasted_iota(jnp.int32, (prow, 1), 0)
    p_ae = p_i >> bits
    p_slot = p_i & (chunk - 1)
    p_a = sum((p_ae >= 3 * m).astype(jnp.int32) for m in (1, 2, 3))
    p_e = jnp.where(p_ae >= 9, 3, p_ae - 3 * p_a)
    e_col = lax.broadcasted_iota(jnp.int32, (prow, chunk * 8), 1)

    def expand(component):
        want = p_slot * 8 + component
        return jnp.concatenate(
            [jnp.where(e_col == want + 4 * ri, 1.0, 0.0) for ri in range(2)], axis=0
        ).astype(BF)

    expand_u = expand(p_a)
    expand_v = expand(p_e)
    s_row = lax.broadcasted_iota(jnp.int32, (chunk * 8, prow), 0)
    s_col = lax.broadcasted_iota(jnp.int32, (chunk * 8, prow), 1)
    s_ae = s_col >> bits
    s_a = sum((s_ae >= 3 * m).astype(jnp.int32) for m in (1, 2, 3))
    s_e = jnp.where(s_ae >= 9, 3, s_ae - 3 * s_a)
    s_same = (s_row >> 3) == (s_col & (chunk - 1))
    s_comp = s_row & 3
    sum_e = jnp.where(s_same & (s_a == s_comp), 1.0, 0.0)
    sum_a = jnp.where(s_same & (s_e == s_comp), 1.0, 0.0)
    none = jnp.zeros((chunk * 8, prow), F32)
    sums = jnp.concatenate(
        [
            jnp.concatenate([sum_e, sum_e, none, none], axis=1),
            jnp.concatenate([none, none, sum_a, sum_a], axis=1),
        ],
        axis=0,
    ).astype(BF)
    lane = lax.broadcasted_iota(jnp.int32, (prow, 2 * LAG), 1)
    lag = jnp.where(lane < LAG, lane, 2 * LAG - lane)
    in_window = (lag >= NT // 32) & (lag < NT // 4)

    def prepare(at):
        if prow > 9 * chunk:
            obsf[9 * chunk :, :] = jnp.zeros((prow - 9 * chunk, 2 * LAG), F32)
        for a in range(3):
            for e in range(3):
                slab = obs[a, e, pl.ds(at * chunk, chunk), :] if chunks > 1 else obs[a, e]
                at_row = (3 * a + e) * chunk
                obsf[at_row : at_row + chunk, :LAG] = slab[:, :LAG].astype(F32)
                obsf[at_row : at_row + chunk, LAG:] = slab[:, NT - LAG :].astype(F32)

    loads[2].wait()
    if chunks == 1:
        prepare(0)

    many(g_send, g_recv, n_b - 1, g_ss, g_rs).wait_recv()
    row_send[...] = jnp.dot(
        g_recv[...].reshape(n_b * rows, cols), station_rows, preferred_element_type=F32
    ).astype(BF).reshape(n_b, rows, band)

    def row_copy(block, slot):
        return pltpu.make_async_remote_copy(
            src_ref=row_send.at[block], dst_ref=row_recv.at[slot], send_sem=row_ss,
            recv_sem=row_rs, device_id=(block, home), device_id_type=MESH,
        )

    mine = q * per + slot_in

    def row_start(step):
        row_copy(wrap(b + 1 + step, n_b), mine).start()

    loop(n_b - 1, row_start)

    @pl.when(q != home)
    def _():
        row_copy(b, mine).start()

    @pl.when(q == home)
    def _():
        row_recv[mine] = row_send[b]

    turn_i = lax.broadcasted_iota(jnp.int32, (cols, cols), 0)
    turn_j = lax.broadcasted_iota(jnp.int32, (cols, cols), 1)
    eye = jnp.where(turn_i == turn_j, 1.0, 0.0).astype(BF)

    def turned(matrix):
        return lax.dot_general(
            eye, matrix[...].reshape(n_b * rows, cols), (((1,), (1,)), ((), ())),
            preferred_element_type=F32,
        ).astype(BF)

    g_turn[0] = turned(g_recv)
    g_turn[1] = turned(g_own)
    many(own_send, own_recv, n_q - 1, own_ss, own_rs).wait_recv()

    def spread(matrix, parts):
        both = jnp.dot(matrix, jnp.concatenate(parts, axis=1), preferred_element_type=F32)
        return both[:prow], both[prow:]

    def spread_own(at):
        return spread(
            expand_u,
            [own_recv[p, pl.ds(at * chunk * 8, chunk * 8), :] for p in range(n_q)],
        )

    def first_part(at):
        alive = jnp.zeros((prow, 1), jnp.int32)
        for i in range(chunk):
            count = cnt_ref[0, q * per + at * blocks + i // cap]
            live = jnp.clip(count - i % cap, 0, 1)
            alive = jnp.where(p_slot == i, live, alive)
        alive = jnp.where(p_ae < 9, alive, 0)
        alive_f = alive.astype(F32)
        keep = in_window & (alive > 0)
        ur, ui = spread_own(at)
        return ur, ui, alive_f, keep

    early = first_part(0) if chunks == 1 else None
    wait_block(
        lambda count: many(row_send, row_recv, count, row_ss, row_rs), lambda c: c.wait_recv()
    )
    for load in loads[3:]:
        load.wait()

    def far_copy(peer, inner, slot):
        return pltpu.make_async_remote_copy(
            src_ref=far_send.at[peer * per + inner], dst_ref=far_recv.at[slot],
            send_sem=far_ss, recv_sem=far_rs,
            device_id=(q * per + inner, peer), device_id_type=MESH,
        )

    def ownt_copy(peer, slot):
        return pltpu.make_async_remote_copy(
            src_ref=ownt_send.at[peer], dst_ref=ownt_recv.at[slot], send_sem=ownt_ss,
            recv_sem=ownt_rs, device_id=(b, peer), device_id_type=MESH,
        )

    def send_quarter(peer):
        def far_start(inner):
            other = jnp.logical_or(q * per + inner != b, q != peer)

            @pl.when(other)
            def _():
                far_copy(peer, inner, b).start()

            @pl.when(jnp.logical_not(other))
            def _():
                far_recv[b] = far_send[peer * per + inner]

        loop(per, far_start)

        @pl.when(q != peer)
        def _():
            ownt_copy(peer, q).start()

        @pl.when(q == peer)
        def _():
            ownt_recv[peer] = ownt_send[peer]

    def work(at):
        if chunks > 1:
            prepare(at)
        ur, ui, alive_f, keep = early if chunks == 1 else first_part(at)
        vr, vi = spread(
            expand_v,
            [
                row_recv[pl.ds(p * per + at * blocks, blocks)].reshape(chunk * 8, band)
                for p in range(n_q)
            ],
        )
        cross = jnp.concatenate(
            [(ur * vr + ui * vi) * alive_f, (ui * vr - ur * vi) * alive_f], axis=1
        ).astype(BF)
        correlation = jnp.concatenate(
            [
                jnp.dot(cross, high[:, :LAG], preferred_element_type=F32),
                jnp.dot(cross, high[:, NT - LAG :], preferred_element_type=F32),
            ],
            axis=1,
        )
        residual = jnp.where(keep, correlation - obsf[...], 0.0).astype(BF)
        adj = jnp.dot(residual, kept[...], preferred_element_type=F32).astype(BF).astype(F32)
        ar, ai = adj[:, :NF], adj[:, NF:]

        def halves(real, imag):
            terms = jnp.concatenate([real, imag], axis=1)
            upper = terms.astype(BF)
            return [upper, (terms - upper.astype(F32)).astype(BF)]

        terms = jnp.concatenate(
            halves(ar * vr - ai * vi, ar * vi + ai * vr)
            + halves(ar * ur + ai * ui, ar * ui - ai * ur),
            axis=0,
        )
        grad = jnp.dot(sums, terms, preferred_element_type=F32)
        top = grad.astype(BF)
        rest = (grad - top.astype(F32)).astype(BF)
        stacked = jnp.concatenate([top, rest], axis=0)
        count = chunk * 16
        first_half = (lax.broadcasted_iota(jnp.int32, (count, half), 0) & 7) < 4
        for peer in range(n_q):
            at_col = peer * 2 * half
            product = jnp.dot(
                stacked, high[:, at_col : at_col + 2 * half], preferred_element_type=F32
            )
            product = (product[:count] + product[count:]) * scale
            message = jnp.where(first_half, product[:, :half], product[:, half:])
            ownt_send[peer, pl.ds(at * chunk * 8, chunk * 8), :] = message[: chunk * 8].astype(BF)
            far_send[pl.ds(peer * per + at * blocks, blocks)] = (
                message[chunk * 8 :].astype(BF).reshape(blocks, rows, half)
            )
            if chunks == 1:
                send_quarter(peer)

    if chunks == 1:
        work(0)
    else:

        def work_step(at, carry):
            work(at)
            return carry

        lax.fori_loop(0, chunks, work_step, 0)
        for peer in range(n_q):
            send_quarter(peer)

    def scatter(matrix, values):
        return jnp.dot(matrix, values, preferred_element_type=F32)

    many(ownt_send, ownt_recv, n_q - 1, ownt_ss, ownt_rs).wait_recv()
    own_sum = scatter(g_turn[1], ownt_recv[...].reshape(n_q * item * 8, half))
    wait_block(
        lambda count: many(far_send, far_recv, count, far_ss, far_rs), lambda c: c.wait_recv()
    )
    summed = own_sum + scatter(g_turn[0], far_recv[...].reshape(n_b * rows, half))
    for h in range(2):
        at_row = h * 4 * sta
        out_ref[:, :, h * half : (h + 1) * half] = summed[at_row : at_row + 3 * sta].reshape(
            3, sta, half
        )

    many(g_send, g_recv, n_b - 1, g_ss, g_rs).wait_send()
    many(own_send, own_recv, n_q - 1, own_ss, own_rs).wait_send()
    many(ownt_send, ownt_recv, n_q - 1, ownt_ss, ownt_rs).wait_send()
    wait_block(
        lambda count: many(row_send, row_recv, count, row_ss, row_rs), lambda c: c.wait_send()
    )
    wait_block(
        lambda count: many(far_send, far_recv, count, far_ss, far_rs), lambda c: c.wait_send()
    )


def local(spectra, observed, own_station, partner_station, pair_count):
    n_b = lax.axis_size("blk")
    n_q = lax.axis_size("frq")
    sta = spectra.shape[2]
    band = spectra.shape[3]
    cap = own_station.shape[2]
    item = observed.shape[0]
    per = n_b // n_q
    rows = cap * 8
    cols = 8 * sta
    half = NT // n_q // 2
    chunk = min(item, 16)
    prow = -(-9 * chunk // 16) * 16
    scale = 1.0 / math.sqrt(2.0 * n_b * cap / sta)
    high, kept = tables()
    dma = pltpu.SemaphoreType.DMA
    held = pl.BlockSpec(memory_space=pltpu.HBM)
    out = pl.pallas_call(
        functools.partial(kernel, n_b, n_q, cap, sta, item, scale),
        out_shape=jax.ShapeDtypeStruct((3, sta, 2 * half), F32),
        in_specs=[held] * 7,
        out_specs=pl.BlockSpec(memory_space=pltpu.VMEM),
        scratch_shapes=[
            pltpu.SMEM((cap, n_b), jnp.int32),
            pltpu.SMEM((cap, n_b), jnp.int32),
            pltpu.SMEM((1, n_b), jnp.int32),
            pltpu.VMEM((2, 4, sta, band), BF),
            pltpu.VMEM((3, 3, item, NT), BF),
            pltpu.VMEM(high.shape, BF),
            pltpu.VMEM(kept.shape, BF),
            pltpu.VMEM((prow, 2 * LAG), F32),
            pltpu.VMEM((n_b, rows, cols), BF),
            pltpu.VMEM((n_b, rows, cols), BF),
            pltpu.VMEM((n_b, rows, cols), BF),
            pltpu.VMEM((2, cols, n_b * rows), BF),
            pltpu.VMEM((n_q, item * 8, band), BF),
            pltpu.VMEM((n_q, item * 8, band), BF),
            pltpu.VMEM((n_b, rows, band), BF),
            pltpu.VMEM((n_q * per, rows, band), BF),
            pltpu.VMEM((n_q * per, rows, half), BF),
            pltpu.VMEM((n_b, rows, half), BF),
            pltpu.VMEM((n_q, item * 8, half), BF),
            pltpu.VMEM((n_q, item * 8, half), BF),
            dma((9,)),
            *[dma(())] * 10,
        ],
        compiler_params=pltpu.CompilerParams(
            collective_id=0, has_side_effects=True, vmem_limit_bytes=32 * 1024 * 1024
        ),
        cost_estimate=pl.CostEstimate(flops=400_000_000, bytes_accessed=6_000_000, transcendentals=0),
    )(
        *(
            pltpu.with_memory_space_constraint(operand, pltpu.HBM)
            for operand in (
                spectra,
                jnp.transpose(observed, (1, 2, 0, 3)),
                jnp.transpose(own_station[0], (1, 0)),
                jnp.transpose(partner_station[0], (1, 0)),
                pair_count,
                jnp.asarray(high),
                jnp.asarray(kept),
            )
        )
    )
    return jnp.transpose(out, (2, 0, 1))


def solution(mesh):
    return jax.shard_map(
        local,
        mesh=mesh,
        in_specs=(
            P(None, None, "blk", "frq"),
            P(("blk", "frq"), None, None, None),
            P("blk", None, None),
            P("blk", None, None),
            P("blk", None),
        ),
        out_specs=P("frq", None, "blk"),
        check_vma=False,
    )
```
